32 devices in a mesh: rcv: 8 (over z, y), src: 4 (over x, core).
Axes of the slice: x: 2, y: 2, z: 4, core: 2. Of those that a mesh axis runs over, the one named last changes fastest.
Arguments:
- rb_data: float32 [32, 64, 512], P('rcv', 'src'), may hold values from -6 to 6
- bs_data: float32 [64, 64, 512], P('rcv', 'src'), may hold values from -0.046875 to 0.046875
- recorded: float32 [32, 64, 512], P('rcv', 'src'), may hold values from -6 to 6
- filters: float32 [3, 21, 32, 64], P(None, None, 'rcv', 'src'), may hold values from -0.9 to 0.9
- offsets: int32 [21], replicated, may hold values from -20 to 20, as said below
Outputs:
- primaries: float32 [32, 64, 512], P('rcv', 'src')
The draws below stay inside these ranges and needn't reach their ends.
Inputs may be any that keep to these rules, and one draw needn't show every extreme that they name: The 21 offsets are distinct, and both -20 and 20 are among them.
All inputs are finite; a program needn't handle non-finite values.
Results may differ from the reference program's by a relative error of at most 0.000073.
Values sent between devices are 32-bit elements; how exact they have to be, the bound alone decides.
No kernel may reach another device: no remote copies, remote signals or barrier semaphores. Data moves between devices by JAX's collectives and lax.ppermute only.
A program may use at most 64 MiB of HBM per device.

```python
import math
import jax
import jax.numpy as jnp
from jax import lax

BOUNCES = 64
SAMPLES = 512
TAPS = 21
LAG = 20
RECEIVERS = 32
SOURCES = 64


def draw_offsets(key, part):
    inner = jax.random.permutation(key, 2 * LAG - 1).astype(jnp.int32) - (LAG - 1)
    ends = jnp.array([-LAG, LAG], jnp.int32)
    return jnp.concatenate([ends, inner[:TAPS - 2]])


def block_levels(own_key, dims, cuts, smallest, largest):
    loudness, own = 1.0, jax.random.fold_in(own_key, 6)
    for axis_at, shards_of in cuts:
        heights = jnp.exp(jax.random.uniform(jax.random.fold_in(own, axis_at), (shards_of,), jnp.float32, smallest / len(cuts), largest / len(cuts)))
        loudness = loudness * jnp.repeat(heights, dims[axis_at] // shards_of).reshape([-1 if axis == axis_at else 1 for axis in range(len(dims))])
    return loudness


def centred(own_key, extent, deviation, reach, cuts=(), held_as=jnp.bfloat16):
    values = jax.random.normal(own_key, extent, jnp.float32) * deviation
    if len(cuts) > 0:
        values = block_levels(own_key, extent, cuts, -0.22, 0.18) * values
    return jnp.clip(values, min=-reach, max=reach).astype(held_as)


def setup_inputs(seed: int = 0) -> dict:
    streams_of = jax.random.split(jax.random.key(seed), 6)
    return {
        "rb_data": centred(streams_of[0], (RECEIVERS, BOUNCES, SAMPLES), 1.0, 6.0, ((0, 8), (1, 4)), jnp.float32),
        "bs_data": centred(streams_of[1], (BOUNCES, SOURCES, SAMPLES), (BOUNCES * SAMPLES // 2) ** -0.5, 0.046875, ((0, 8), (1, 4)), jnp.float32),
        "recorded": centred(streams_of[2], (RECEIVERS, SOURCES, SAMPLES), 1.0, 6.0, ((0, 8), (1, 4)), jnp.float32),
        "filters": centred(streams_of[3], (3, TAPS, RECEIVERS, SOURCES), 0.15, 0.9, ((2, 8), (3, 4)), jnp.float32),
        "offsets": draw_offsets(jax.random.fold_in(streams_of[5], 71), 0),
    }


def predict(rb_data, bs_data):
    length = 2 * SAMPLES
    left = jnp.fft.rfft(rb_data, n=length, axis=-1)
    right = jnp.fft.rfft(bs_data, n=length, axis=-1)
    block = math.gcd(RECEIVERS, 16)
    groups = left.reshape(RECEIVERS // block, block, BOUNCES, SAMPLES + 1)

    def one_group(group):
        product = jnp.einsum('rbf,bsf->rsf', group, right)
        return jnp.fft.irfft(product, n=length, axis=-1)[..., :SAMPLES]

    result = lax.map(one_group, groups)
    return result.reshape(RECEIVERS, SOURCES, SAMPLES).astype(rb_data.dtype)


def reference(rb_data, bs_data, recorded, filters, offsets):
    prediction = predict(rb_data, bs_data)
    padded = jnp.pad(prediction, ((1, 1), (0, 0), (LAG, LAG)))

    def tap_step(index, total):
        shift = offsets[index]
        window = lax.dynamic_slice_in_dim(padded, (LAG - shift).astype(jnp.int32), SAMPLES, 2)
        weights = lax.dynamic_index_in_dim(filters, index, 1, keepdims=False)
        for row in range(3):
            total = total + weights[row][:, :, None] * window[row:row + RECEIVERS]
        return total

    total = lax.fori_loop(0, TAPS, tap_step, jnp.zeros_like(recorded))
    return recorded - total
```

```python
import functools
import math

import jax
import jax.numpy as jnp
import ml_dtypes
import numpy as np
from jax import lax
from jax.experimental import pallas as pl
from jax.experimental.pallas import tpu as pltpu
from jax.sharding import PartitionSpec as P

LANES = 128
SUBLANES = 8
VMEM_LIMIT = 40 * 1024 * 1024
AXES = ("rcv", "src")
GROUP = 4


def halves(table):
    high = table.astype(np.float32).astype(ml_dtypes.bfloat16)
    low = (table - high.astype(np.float64)).astype(np.float32).astype(ml_dtypes.bfloat16)
    return high, low


def dft_tables(samples):
    times = np.arange(samples, dtype=np.int64)[:, None]
    odd = 2 * np.arange(samples, dtype=np.int64)[None, :] + 1
    phase = (times * odd % (4 * samples)).astype(np.float64) * (math.pi / (2 * samples))
    cosine, sine = np.cos(phase), np.sin(phase)
    forward = np.concatenate([cosine, -sine], axis=1)
    inverse = np.concatenate([cosine.T, -sine.T], axis=0) / samples
    return halves(forward) + halves(inverse)


def split_dot(rows, high_table, low_table):
    high = rows.astype(jnp.bfloat16)
    low = (rows - high.astype(jnp.float32)).astype(jnp.bfloat16)
    dot = functools.partial(jnp.dot, preferred_element_type=jnp.float32)
    return dot(high, high_table) + (dot(low, high_table) + dot(high, low_table))


def spectra(traces_ref, tables):
    lead = traces_ref.shape[:-1]
    samples = traces_ref.shape[-1]
    rows = math.prod(lead)
    return split_dot(traces_ref[...].reshape(rows, samples), *tables).reshape(lead + (2 * samples,))


def add_products(total_ref, lefts, right_ref, place, begin=True):
    _, sources, width = total_ref.shape
    half = width // 2
    for tile in range(half // LANES):
        real = pl.ds(tile * LANES, LANES)
        imag = pl.ds(half + tile * LANES, LANES)
        for group in range(0, len(lefts), GROUP):
            members = lefts[group : group + GROUP]
            if begin:
                zero = jnp.zeros((sources, LANES), jnp.float32)
                sums = [(zero, zero) for _ in members]
            else:
                sums = [(total_ref[row, :, real], total_ref[row, :, imag]) for row, _, _ in members]
            for bounce in range(right_ref.shape[0]):
                at = place(bounce)
                right_real = right_ref[bounce, :, real]
                right_imag = right_ref[bounce, :, imag]
                for index, (_, left_ref, row) in enumerate(members):
                    left_real = left_ref[at, row : row + 1, real]
                    left_imag = left_ref[at, row : row + 1, imag]
                    sum_real, sum_imag = sums[index]
                    sums[index] = (
                        sum_real + (left_real * right_real - left_imag * right_imag),
                        sum_imag + (left_real * right_imag + left_imag * right_real),
                    )
            for index, (row, _, _) in enumerate(members):
                total_ref[row, :, real], total_ref[row, :, imag] = sums[index]


def to_traces(prediction_ref, total_ref, tables):
    rows, sources, width = total_ref.shape
    flat = total_ref[...].reshape(rows * sources, width)
    prediction_ref[...] = split_dot(flat, *tables).reshape(prediction_ref.shape)


def matched(store, prediction_ref, weights_ref, offsets_ref):
    extended, sources, samples = prediction_ref.shape
    receivers = extended - 2
    taps = offsets_ref.shape[0]
    tiles = samples // LANES
    lane = lax.broadcasted_iota(jnp.int32, (SUBLANES, LANES), 1)
    for part in range(sources // SUBLANES):
        which = pl.ds(part * SUBLANES, SUBLANES)
        zero = jnp.zeros((SUBLANES, LANES), jnp.float32)
        sums = [[zero] * tiles for _ in range(receivers)]
        for tap in range(taps):
            offset = offsets_ref[tap]
            later = offset < 0
            turn = jnp.where(later, offset + LANES, offset)
            from_before = lane < jnp.where(later, 0, turn)
            from_after = lane >= jnp.where(later, turn, LANES)
            for row in range(extended):
                turned = [
                    pltpu.roll(prediction_ref[row, which, pl.ds(t * LANES, LANES)], turn, 1)
                    for t in range(tiles)
                ]
                turned = [zero] + turned + [zero]
                shifted = [
                    jnp.where(
                        from_before,
                        turned[t],
                        jnp.where(from_after, turned[t + 2], turned[t + 1]),
                    )
                    for t in range(tiles)
                ]
                for near in range(3):
                    receiver = row - near
                    if 0 <= receiver < receivers:
                        at = (near * receivers + receiver) * taps + tap
                        weight = jnp.broadcast_to(
                            weights_ref[which, at : at + 1], (SUBLANES, LANES)
                        )
                        for t in range(tiles):
                            sums[receiver][t] = sums[receiver][t] + weight * shifted[t]
        for receiver in range(receivers):
            for t in range(tiles):
                store(receiver, which, pl.ds(t * LANES, LANES), sums[receiver][t])


def place_of(where_ref, slots, left_count, right_count, first):
    row, column = where_ref[0], where_ref[1]

    def place(index):
        block, rest = first + index // right_count, index % right_count
        bounce = jnp.bitwise_xor(row, block) * right_count + rest
        holder = (bounce // left_count) % slots
        return jnp.bitwise_xor(holder, column % slots) * left_count + bounce % left_count

    return place


def weights_kernel(filters_ref, out_ref):
    near, receivers, _, taps = filters_ref.shape
    for step in range(near):
        for receiver in range(receivers):
            at = (step * receivers + receiver) * taps
            out_ref[:, at : at + taps] = filters_ref[step, receiver]


def pack_kernel(slots, where_ref, *refs):
    out_ref, firsts_ref, lasts_ref = refs[3 * slots :]
    same = where_ref[2] == 1
    receivers, count, _ = refs[0].shape
    for slot in range(slots):
        here, one, two = refs[3 * slot : 3 * slot + 3]
        which = pl.ds(slot * count, count)
        for row in range(receivers):
            own = jnp.where(same, here[row], one[row])
            mirror = jnp.where(same, one[row], two[row])
            out_ref[which, row, :] = own
            out_ref[which, receivers + row, :] = mirror
            for ref, edge in ((firsts_ref, 0), (lasts_ref, receivers - 1)):
                if row == edge:
                    ref[0, which] = own
                    ref[1, which] = mirror


def first_kernel(slots, blocks, *refs):
    where_ref, high_ref, low_ref, traces_ref = refs[:4]
    right_refs = refs[4 : 4 + blocks]
    left_ref, right_spectra, total_ref = refs[4 + blocks :]
    tables = (high_ref[...], low_ref[...])
    right_count = right_refs[0].shape[0]
    for block, ref in enumerate(right_refs):
        right_spectra[pl.ds(block * right_count, right_count)] = spectra(ref, tables)
    left_ref[...] = spectra(traces_ref, tables)
    place = place_of(where_ref, slots, left_ref.shape[0] // slots, right_count, 0)
    lefts = [(row, left_ref, row) for row in range(left_ref.shape[1])]
    add_products(total_ref, lefts, right_spectra, place)


def halo_spectra(out_ref, rows_ref, scratch, tables):
    for row in range(rows_ref.shape[0]):
        scratch[:, row, :] = rows_ref[row]
    count, padded, samples = scratch.shape
    flat = scratch[...].reshape(count * padded, samples)
    out_ref[...] = split_dot(flat, *tables).reshape(out_ref.shape)


def partial_traces(
    first_row, block, slots, where_ref, total, prediction, tables, left_ref, halo_ref, halos,
    start_ref, early_ref, late_ref,
):
    receivers = prediction.shape[0] - 2
    left_count = left_ref.shape[0] // slots
    right_count = late_ref.shape[0]
    early = place_of(where_ref, slots, left_count, right_count, 0)
    late = place_of(where_ref, slots, left_count, right_count, block)
    rows = [(1 + row, left_ref, first_row + row) for row in range(receivers)]
    outer = [(0, halo_ref, halos[0]), (receivers + 1, halo_ref, halos[1])]
    total[pl.ds(1, receivers)] = start_ref[pl.ds(first_row, receivers)]
    add_products(total, rows, late_ref, late, begin=False)
    add_products(total, outer, early_ref, early)
    add_products(total, outer, late_ref, late, begin=False)
    to_traces(prediction, total, tables)


def mirror_kernel(
    block, slots, where_ref, offsets_ref, high_ref, low_ref, back_high_ref, back_low_ref,
    right_ref, left_ref, before_ref, after_ref, start_ref, early_ref, weights_ref,
    out_ref, late_ref, halo_ref, total, prediction, halo_rows, halo_turned,
):
    row = where_ref[0]
    lower = row < block + 1
    first, last = row % (block + 1) == 0, row % (block + 1) == block
    zero = jnp.zeros(before_ref.shape[1:], jnp.float32)
    for which, (ref, end, none) in enumerate(
        ((before_ref, first, lower), (after_ref, last, jnp.logical_not(lower)))
    ):
        own, mirror = ref[0], ref[1]
        halo_rows[which] = jnp.where(end, jnp.where(none, zero, mirror), own)
        halo_rows[2 + which] = jnp.where(end, jnp.where(none, own, zero), mirror)
    tables = (high_ref[...], low_ref[...])
    late_ref[...] = spectra(right_ref, tables)
    halo_spectra(halo_ref, halo_rows, halo_turned, tables)
    receivers = out_ref.shape[0]
    partial_traces(
        receivers, block, slots, where_ref, total, prediction,
        (back_high_ref[...], back_low_ref[...]), left_ref, halo_ref, (2, 3),
        start_ref, early_ref, late_ref,
    )

    def store(receiver, which, times, value):
        out_ref[receiver, which, times] = value

    matched(store, prediction, weights_ref, offsets_ref)


def own_kernel(
    block, slots, where_ref, offsets_ref, back_high_ref, back_low_ref, left_ref, halo_ref,
    start_ref, early_ref, late_ref, weights_ref, recorded_ref, out_ref, total, prediction,
):
    partial_traces(
        0, block, slots, where_ref, total, prediction, (back_high_ref[...], back_low_ref[...]),
        left_ref, halo_ref, (0, 1), start_ref, early_ref, late_ref,
    )

    def store(receiver, which, times, value):
        out_ref[receiver, which, times] = recorded_ref[receiver, which, times] - value

    matched(store, prediction, weights_ref, offsets_ref)


def last_kernel(part_ref, arrived_ref, out_ref):
    out_ref[...] = part_ref[...] - arrived_ref[...]


def call(kernel, scalars, arrays, out_shapes, scratch, flops):
    shapes = [jax.ShapeDtypeStruct(shape, jnp.float32) for shape in out_shapes]
    vmem = pl.BlockSpec(memory_space=pltpu.VMEM)
    moved = sum(a.size * a.dtype.itemsize for a in arrays) + sum(4 * math.prod(s) for s in out_shapes)
    return pl.pallas_call(
        kernel,
        out_shape=shapes,
        in_specs=[pl.BlockSpec(memory_space=pltpu.SMEM)] * len(scalars) + [vmem] * len(arrays),
        out_specs=[vmem] * len(shapes),
        scratch_shapes=[pltpu.VMEM(shape, jnp.float32) for shape in scratch],
        compiler_params=pltpu.CompilerParams(vmem_limit_bytes=VMEM_LIMIT),
        cost_estimate=pl.CostEstimate(flops=flops, bytes_accessed=moved, transcendentals=0),
    )(*scalars, *arrays)


def local(rows, columns, rb_data, bs_data, recorded, filters, offsets):
    receivers, left_count, samples = rb_data.shape
    right_count, sources, _ = bs_data.shape
    near, taps = filters.shape[:2]
    slots, blocks = columns // 2, rows // 2
    row, column = lax.axis_index("rcv"), lax.axis_index("src")
    same = row // blocks == column // slots
    where = jnp.stack([row, column, same]).astype(jnp.int32)

    def permute(array, target):
        pairs = []
        for i in range(rows):
            for j in range(columns):
                to = target(i, j)
                if to is not None and 0 <= to[0] < rows:
                    pairs.append((i * columns + j, to[0] * columns + to[1]))
        return lax.ppermute(array, AXES, pairs)

    def is_same(i, j):
        return i // blocks == j // slots

    one = permute(
        rb_data, lambda i, j: (i, j ^ slots) if is_same(i, j) else (i ^ blocks, j)
    )
    right = [bs_data] + [
        permute(bs_data, lambda i, j, k=k: (i ^ k, j)) for k in range(1, blocks)
    ]
    two = permute(one, lambda i, j: (i, j ^ slots) if is_same(i, j) else None)
    left = [rb_data, one, two]
    for k in range(1, slots):
        left += [permute(part, lambda i, j, k=k: (i, j ^ k)) for part in (rb_data, one)]
        left.append(permute(two, lambda i, j, k=k: None if is_same(i, j) else (i, j ^ k)))

    by_tap = filters.transpose(0, 2, 3, 1)
    (weights,) = call(
        weights_kernel, [], [by_tap],
        [(sources, -(-near * receivers * taps // LANES) * LANES)], [], 0,
    )
    mirror_weights = permute(weights, lambda i, j: (i ^ blocks, j))

    high, low, back_high, back_low = [jnp.asarray(t) for t in dft_tables(samples)]
    width = 2 * samples
    held = slots * left_count
    edge_shape = (2, held, samples)
    traces, firsts, lasts = call(
        functools.partial(pack_kernel, slots), [where], left,
        [(held, 2 * receivers, samples), edge_shape, edge_shape], [], 0,
    )
    after = permute(firsts, lambda i, j: ((i - 1) % blocks + i // blocks * blocks, j))
    before = permute(lasts, lambda i, j: ((i + 1) % blocks + i // blocks * blocks, j))
    mac = 6 * samples * width
    early_shape = ((blocks - 1) * right_count, sources, width)
    late_shape = (right_count, sources, width)
    left_spectra, early, total = call(
        functools.partial(first_kernel, slots, blocks - 1),
        [where],
        [high, low, traces] + right[:-1],
        [(held, 2 * receivers, width), early_shape, (2 * receivers, sources, width)],
        [],
        mac * (2 * receivers * held + (blocks - 1) * right_count * sources),
    )
    halo_shape = (held, SUBLANES, width)
    scratch = [(receivers + 2, sources, width), (receivers + 2, sources, samples)]
    mirror_part, late, halo = call(
        functools.partial(mirror_kernel, blocks - 1, slots),
        [where, offsets],
        [high, low, back_high, back_low, right[-1], left_spectra, before, after, total, early,
         mirror_weights],
        [recorded.shape, late_shape, halo_shape],
        scratch + [(4, held, samples), (held, SUBLANES, samples)],
        mac * (right_count + receivers) * sources,
    )
    arrived = permute(mirror_part, lambda i, j: (i ^ blocks, j))
    (own_part,) = call(
        functools.partial(own_kernel, blocks - 1, slots),
        [where, offsets],
        [back_high, back_low, left_spectra, halo, total, early, late, weights, recorded],
        [recorded.shape],
        scratch,
        mac * receivers * sources,
    )
    (out,) = call(last_kernel, [], [own_part, arrived], [recorded.shape], [], 0)
    return out


def solution(mesh):
    in_specs = (
        P("rcv", "src", None),
        P("rcv", "src", None),
        P("rcv", "src", None),
        P(None, None, "rcv", "src"),
        P(),
    )
    out_specs = P("rcv", "src", None)
    body = functools.partial(local, mesh.shape["rcv"], mesh.shape["src"])
    return jax.shard_map(body, mesh=mesh, in_specs=in_specs, out_specs=out_specs, check_vma=False)
```

```python
import functools
import math

import jax
import jax.numpy as jnp
import numpy as np
from jax import lax
from jax.experimental import pallas as pl
from jax.experimental.pallas import tpu as pltpu
from jax.sharding import PartitionSpec as P

LANES = 128
SUBLANES = 8
VMEM_LIMIT = 40 * 1024 * 1024
AXES = ("rcv", "src")
STEP = 32
GROUP = 4
CHUNK = 64


def phases(samples):
    fine = np.arange(STEP, dtype=np.int64)
    coarse = np.arange(0, samples, STEP, dtype=np.int64)
    times = np.concatenate([coarse, fine])[:, None]
    odd = 2 * np.arange(samples, dtype=np.int64)[None, :] + 1
    phase = (times * odd % (4 * samples)).astype(np.float64) * (math.pi / (2 * samples))
    return np.concatenate([np.cos(phase), np.sin(phase)], axis=0).astype(np.float32)


def dft_tables(high_ref, low_ref, phases_ref):
    samples = high_ref.shape[0]
    coarse = samples // STEP
    half = phases_ref.shape[0] // 2
    cos_fine = phases_ref[coarse:half]
    sin_fine = phases_ref[half + coarse :]
    for step in range(coarse):
        cos_step = phases_ref[step : step + 1]
        sin_step = phases_ref[half + step : half + step + 1]
        cosine = cos_step * cos_fine - sin_step * sin_fine
        sine = sin_step * cos_fine + cos_step * sin_fine
        for value, at in ((cosine, 0), (-sine, samples)):
            high = value.astype(jnp.bfloat16)
            where = (pl.ds(step * STEP, STEP), pl.ds(at, samples))
            high_ref[where] = high
            low_ref[where] = (value - high.astype(jnp.float32)).astype(jnp.bfloat16)


def split_dot(rows, high_table, low_table, of=0):
    high = rows.astype(jnp.bfloat16)
    low = (rows - high.astype(jnp.float32)).astype(jnp.bfloat16)

    def dot(left, right):
        return lax.dot_general(
            left, right, (((1,), (of,)), ((), ())), preferred_element_type=jnp.float32
        )

    return dot(high, high_table) + (dot(low, high_table) + dot(high, low_table))


def spectra(traces_ref, tables):
    lead = traces_ref.shape[:-1]
    samples = traces_ref.shape[-1]
    rows = math.prod(lead)
    return split_dot(traces_ref[...].reshape(rows, samples), *tables).reshape(lead + (2 * samples,))


def with_sums(values):
    half = values.shape[-1] // 2
    total = values[..., :half] + values[..., half:]
    return jnp.concatenate([values, total], axis=-1)


def products(total_ref, lefts, right_ref):
    _, sources, width = total_ref.shape
    half = width // 2
    zero = jnp.zeros((sources, LANES), jnp.float32)
    for tile in range(half // LANES):
        real = pl.ds(tile * LANES, LANES)
        imag = pl.ds(half + tile * LANES, LANES)
        both = pl.ds(width + tile * LANES, LANES)
        for group in range(0, len(lefts), GROUP):
            members = lefts[group : group + GROUP]
            sums = [(zero, zero, zero) for _ in members]
            for bounce in range(right_ref.shape[0]):
                at = slice(bounce, bounce + 1)
                right_real = right_ref[bounce, :, real]
                right_imag = right_ref[bounce, :, imag]
                right_more = right_imag - right_real
                right_both = right_imag + right_real
                for index, (_, left_ref, row) in enumerate(members):
                    one, two, three = sums[index]
                    sums[index] = (
                        one + left_ref[row, at, both] * right_real,
                        two + left_ref[row, at, real] * right_more,
                        three + left_ref[row, at, imag] * right_both,
                    )
            for (one, two, three), (row, _, _) in zip(sums, members):
                total_ref[row, :, real] = one - three
                total_ref[row, :, imag] = one + two


def to_traces(prediction_ref, total_ref, tables):
    rows, sources, width = total_ref.shape
    flat = total_ref[...].reshape(rows * sources, width) * (2.0 / width)
    prediction_ref[...] = split_dot(flat, *tables, of=1).reshape(prediction_ref.shape)


def lay_weights(weights_ref, scratch, filters_ref):
    near, receivers, sources, taps = filters_ref.shape
    scratch[...] = jnp.zeros(scratch.shape, jnp.float32)
    lanes = receivers * sources
    for copy in range(LANES // lanes):
        for step in range(near):
            for receiver in range(receivers):
                rows = pl.ds(copy * lanes + receiver * sources, sources)
                scratch[rows, step * taps : (step + 1) * taps] = filters_ref[step, receiver]
    weights_ref[...] = scratch[...].T[: weights_ref.shape[0]]


def matched(prediction_ref, weights_ref, offsets_ref, turned, sums):
    extended, sources, samples = prediction_ref.shape
    taps = offsets_ref.shape[0]
    receivers = extended - 2
    lanes = receivers * sources
    parts = LANES // lanes
    per = samples // parts
    zero = jnp.zeros((lanes, LANES), jnp.float32)
    for near in range(3):
        for block in range(per // LANES + 2):
            side = []
            for part in range(parts):
                at = part * per + (block - 1) * LANES
                if 0 <= at < samples:
                    rows = prediction_ref[pl.ds(near, receivers), :, at : at + LANES]
                    side.append(rows.reshape(lanes, LANES))
                else:
                    side.append(zero)
            turned[near, pl.ds(block * LANES, LANES)] = jnp.concatenate(side, axis=0).T
    chunk = min(per, CHUNK)
    for first in range(0, per, chunk):
        total = jnp.zeros((chunk, LANES), jnp.float32)
        for tap in range(taps):
            start = LANES + first - offsets_ref[tap]
            for near in range(3):
                at = near * taps + tap
                total = total + weights_ref[at : at + 1] * turned[near, pl.ds(start, chunk), :]
        sums[pl.ds(first, chunk)] = total
    back = jnp.concatenate(
        [sums[at : at + LANES].T for at in range(0, per, LANES)], axis=1
    ).reshape(parts, receivers, sources, per)
    return jnp.concatenate([back[part] for part in range(parts)], axis=2)


def first_kernel(phases_ref, here_ref, right_ref, high_ref, low_ref, here_out, right_out):
    dft_tables(high_ref, low_ref, phases_ref)
    tables = (high_ref[...], low_ref[...])
    here_out[...] = with_sums(spectra(here_ref, tables))
    right_out[...] = spectra(right_ref, tables)


def second_kernel(high_ref, low_ref, filters_ref, one_ref, *refs):
    right_refs, (weights_ref, one_out, right_out, turned) = refs[:-4], refs[-4:]
    lay_weights(weights_ref, turned, filters_ref)
    tables = (high_ref[...], low_ref[...])
    one_out[...] = with_sums(spectra(one_ref, tables))
    held = right_refs[0].shape[0]
    for block, ref in enumerate(right_refs):
        right_out[pl.ds(block * held, held)] = spectra(ref, tables)


def place_of(column, slot, slots, held):
    first = jnp.bitwise_xor(column, slot) % slots * held
    return pl.ds(pl.multiple_of(first, held), held)


def edge_kernel(slots, where_ref, *refs):
    near_ref, far_ref = refs[3 * slots :]
    odd, column, same = where_ref[0] % 2 == 1, where_ref[1], where_ref[2] == 1
    receivers, held, _ = refs[0].shape
    for slot in range(slots):
        these = place_of(column, slot, slots, held)
        here, one, two = refs[3 * slot : 3 * slot + 3]
        for index, (yes, no) in enumerate(((here, one), (one, two))):
            first = jnp.where(same, yes[0], no[0])
            last = jnp.where(same, yes[receivers - 1], no[receivers - 1])
            near_ref[index, these] = jnp.where(odd, first, last)
            far_ref[index, these] = jnp.where(odd, last, first)


def main_kernel(
    slots, blocks, where_ref, high_ref, low_ref, right_a, right_b, here_ref, one_ref, *refs
):
    columns, refs = refs[: 3 * slots - 2], refs[3 * slots - 2 :]
    right_refs, (total_ref, right_ref, own_ref, left_ref) = refs[:-4], refs[-4:]
    tables = (high_ref[...], low_ref[...])
    row, column, same = where_ref[0], where_ref[1], where_ref[2] == 1
    count = right_a.shape[0]
    block = 0
    for ref, done in ((right_a, True), (right_b, True)) + tuple((r, False) for r in right_refs):
        for first in range(0, ref.shape[0], count):
            value = ref[pl.ds(first, count)] if done else spectra(ref, tables)
            at = jnp.bitwise_xor(row, block) % blocks * count
            right_ref[pl.ds(at, count)] = value
            block += 1
    receivers, held, _ = here_ref.shape
    for slot in range(slots):
        these = place_of(column, slot, slots, held)
        if slot == 0:
            two = with_sums(spectra(columns[0], tables))
            own = jnp.where(same, here_ref[...], one_ref[...])
            mirror = jnp.where(same, one_ref[...], two)
        else:
            here, one, two = [ref[...] for ref in columns[3 * slot - 2 : 3 * slot + 1]]
            chosen = jnp.concatenate([jnp.where(same, here, one), jnp.where(same, one, two)])
            flat = chosen.reshape(2 * receivers * held, chosen.shape[-1])
            value = with_sums(split_dot(flat, *tables)).reshape(2 * receivers, held, -1)
            own, mirror = value[:receivers], value[receivers:]
        for receiver in range(receivers):
            own_ref[receiver, these] = own[receiver]
            left_ref[receiver, these] = mirror[receiver]
    products(total_ref, [(row, left_ref, row) for row in range(receivers)], right_ref)


def mirror_kernel(
    blocks, where_ref, offsets_ref, high_ref, low_ref, weights_ref, near_ref, far_ref,
    start_ref, right_ref, out_ref, halo_ref, total, prediction, turned, sums, outer,
):
    receivers = out_ref.shape[0]
    row = where_ref[0]
    odd, lower = row % 2 == 1, row < blocks
    before = jnp.where(odd, near_ref[...], far_ref[...])
    after = jnp.where(odd, far_ref[...], near_ref[...])
    zero = jnp.zeros(before.shape[1:], jnp.float32)
    for which, (value, end, none) in enumerate(
        (
            (before, row % blocks == 0, lower),
            (after, row % blocks == blocks - 1, jnp.logical_not(lower)),
        )
    ):
        own, mirror = value[0], value[1]
        outer[which] = jnp.where(end, jnp.where(none, zero, mirror), own)
        outer[2 + which] = jnp.where(end, jnp.where(none, own, zero), mirror)
    tables = (high_ref[...], low_ref[...])
    halo_ref[...] = with_sums(spectra(outer, tables))
    total[pl.ds(1, receivers)] = start_ref[...]
    products(total, [(0, halo_ref, 2), (receivers + 1, halo_ref, 3)], right_ref)
    to_traces(prediction, total, tables)
    out_ref[...] = matched(prediction, weights_ref, offsets_ref, turned, sums)


def own_kernel(
    offsets_ref, high_ref, low_ref, weights_ref, right_ref, left_ref, halo_ref, recorded_ref,
    out_ref, total, prediction, turned, sums,
):
    receivers = out_ref.shape[0]
    lefts = [(1 + row, left_ref, row) for row in range(receivers)]
    products(total, [(0, halo_ref, 0)] + lefts + [(receivers + 1, halo_ref, 1)], right_ref)
    to_traces(prediction, total, (high_ref[...], low_ref[...]))
    out_ref[...] = recorded_ref[...] - matched(
        prediction, weights_ref, offsets_ref, turned, sums
    )


def last_kernel(part_ref, arrived_ref, out_ref):
    out_ref[...] = part_ref[...] - arrived_ref[...]


def call(kernel, scalars, arrays, outs, scratch, in_hbm=0):
    shapes = [s if hasattr(s, "dtype") else jax.ShapeDtypeStruct(s, jnp.float32) for s in outs]
    vmem = pl.BlockSpec(memory_space=pltpu.VMEM)
    return pl.pallas_call(
        kernel,
        out_shape=shapes,
        in_specs=[pl.BlockSpec(memory_space=pltpu.SMEM)] * len(scalars)
        + [pl.BlockSpec(memory_space=pltpu.HBM)] * in_hbm
        + [vmem] * (len(arrays) - in_hbm),
        out_specs=[vmem] * len(shapes),
        scratch_shapes=[
            s if not isinstance(s, tuple) else pltpu.VMEM(s, jnp.float32) for s in scratch
        ],
        compiler_params=pltpu.CompilerParams(vmem_limit_bytes=VMEM_LIMIT),
    )(*scalars, *arrays)


def local(rows, columns, rb_data, bs_data, recorded, filters, offsets):
    receivers, left_count, samples = rb_data.shape
    right_count, sources, _ = bs_data.shape
    taps = offsets.shape[0]
    slots, blocks = columns // 2, rows // 2
    row, column = lax.axis_index("rcv"), lax.axis_index("src")
    same = row // blocks == column // slots
    where = jnp.stack([row, column, same]).astype(jnp.int32)

    def permute(array, target):
        pairs = []
        for i in range(rows):
            for j in range(columns):
                to = target(i, j)
                if to is not None and 0 <= to[0] < rows:
                    pairs.append((i * columns + j, to[0] * columns + to[1]))
        return lax.ppermute(array, AXES, pairs)

    def is_same(i, j):
        return i // blocks == j // slots

    def other_rows(first, end):
        return [permute(bs_data, lambda i, j, k=k: (i ^ k, j)) for k in range(first, end)]

    cut = 2 * blocks // 3 + 1
    width = 2 * samples
    held = slots * left_count
    one = permute(
        rb_data, lambda i, j: (i, j ^ slots) if is_same(i, j) else (i ^ blocks, j)
    )
    some = other_rows(1, cut)
    heres = [rb_data] + [
        permute(rb_data, lambda i, j, k=k: (i, j ^ k)) for k in range(1, slots)
    ]
    table = jax.ShapeDtypeStruct((samples, width), jnp.bfloat16)
    left_shape = (receivers, left_count, width + samples)
    high, low, here_spectra, right_a = call(
        first_kernel, [], [jnp.asarray(phases(samples)), rb_data, bs_data],
        [table, table, left_shape, (right_count, sources, width)], [],
    )
    one, some, heres, high, low, here_spectra, right_a = lax.optimization_barrier(
        (one, some, heres, high, low, here_spectra, right_a)
    )
    gathered = []
    for k in range(slots):
        if k > 0:
            gathered.append(heres[k])
            gathered.append(permute(one, lambda i, j, k=k: (i, j ^ k)))
        gathered.append(
            permute(one, lambda i, j, k=k: (i, j ^ slots ^ k) if is_same(i, j) else None)
        )
    rest = other_rows(cut, blocks)
    weights, one_spectra, right_b = call(
        second_kernel, [], [high, low, filters.transpose(0, 2, 3, 1), one] + some,
        [
            (-(-3 * taps // SUBLANES) * SUBLANES, LANES),
            left_shape,
            (len(some) * right_count, sources, width),
        ],
        [(LANES, LANES)],
    )
    gathered, rest, weights, one_spectra, right_b = lax.optimization_barrier(
        (gathered, rest, weights, one_spectra, right_b)
    )
    edge_shape = (2, held, samples)
    near, far = call(
        functools.partial(edge_kernel, slots), [where], [rb_data, one] + gathered,
        [edge_shape, edge_shape], [],
    )

    def in_half(i, at):
        return at % blocks + i // blocks * blocks

    near = permute(near, lambda i, j: (i ^ 1, j))
    far = permute(far, lambda i, j: (in_half(i, i + 1 if i % 2 else i - 1), j))
    mirror_weights = permute(weights, lambda i, j: (i ^ blocks, j))
    per = samples * receivers * sources // LANES
    total, right, own_left = call(
        functools.partial(main_kernel, slots, blocks),
        [where],
        [high, low, right_a, right_b, here_spectra, one_spectra] + gathered + rest,
        [
            (receivers, sources, width),
            (blocks * right_count, sources, width),
            (receivers, held, width + samples),
        ],
        [(receivers, held, width + samples)],
    )
    scratch = [
        (receivers + 2, sources, width),
        (receivers + 2, sources, samples),
        (filters.shape[0], per + 2 * LANES, LANES),
        (per, LANES),
    ]
    mirror_part, halo = call(
        functools.partial(mirror_kernel, blocks),
        [where, offsets],
        [high, low, mirror_weights, near, far, total, right],
        [recorded.shape, (4, held, width + samples)],
        scratch + [(4, held, samples)],
    )
    arrived = permute(mirror_part, lambda i, j: (i ^ blocks, j))
    (own_part,) = call(
        own_kernel, [offsets], [high, low, weights, right, own_left, halo, recorded],
        [recorded.shape], scratch,
    )
    (out,) = call(last_kernel, [], [own_part, arrived], [recorded.shape], [])
    return out


def solution(mesh):
    in_specs = (
        P("rcv", "src", None),
        P("rcv", "src", None),
        P("rcv", "src", None),
        P(None, None, "rcv", "src"),
        P(),
    )
    out_specs = P("rcv", "src", None)
    body = functools.partial(local, mesh.shape["rcv"], mesh.shape["src"])
    return jax.shard_map(body, mesh=mesh, in_specs=in_specs, out_specs=out_specs, check_vma=False)
```

```python
import functools
import math

import jax
import jax.numpy as jnp
import numpy as np
from jax import lax
from jax.experimental import pallas as pl
from jax.experimental.pallas import tpu as pltpu
from jax.sharding import PartitionSpec as P

LANES = 128
SUBLANES = 8
VMEM_LIMIT = 20 * 1024 * 1024
AXES = ("rcv", "src")
STEP = 32
GROUP = 4
CHUNK = 64


def phases(samples):
    fine = np.arange(STEP, dtype=np.int64)
    coarse = np.arange(0, samples, STEP, dtype=np.int64)
    times = np.concatenate([coarse, fine])[:, None]
    odd = 2 * np.arange(samples, dtype=np.int64)[None, :] + 1
    phase = (times * odd % (4 * samples)).astype(np.float64) * (math.pi / (2 * samples))
    return np.concatenate([np.cos(phase), np.sin(phase)], axis=0).astype(np.float32)


def dft_tables(high_ref, low_ref, phases_ref):
    samples = high_ref.shape[0]
    coarse = samples // STEP
    half = phases_ref.shape[0] // 2
    cos_fine = phases_ref[coarse:half]
    sin_fine = phases_ref[half + coarse :]
    for step in range(coarse):
        cos_step = phases_ref[step : step + 1]
        sin_step = phases_ref[half + step : half + step + 1]
        cosine = cos_step * cos_fine - sin_step * sin_fine
        sine = sin_step * cos_fine + cos_step * sin_fine
        for value, at in ((cosine, 0), (-sine, samples)):
            high = value.astype(jnp.bfloat16)
            where = (pl.ds(step * STEP, STEP), pl.ds(at, samples))
            high_ref[where] = high
            low_ref[where] = (value - high.astype(jnp.float32)).astype(jnp.bfloat16)


def split_dot(rows, high_table, low_table, of=0):
    high = rows.astype(jnp.bfloat16)
    low = (rows - high.astype(jnp.float32)).astype(jnp.bfloat16)

    def dot(left, right):
        return lax.dot_general(
            left, right, (((1,), (of,)), ((), ())), preferred_element_type=jnp.float32
        )

    return dot(high, high_table) + (dot(low, high_table) + dot(high, low_table))


def spectra(traces_ref, tables):
    lead = traces_ref.shape[:-1]
    samples = traces_ref.shape[-1]
    rows = math.prod(lead)
    return split_dot(traces_ref[...].reshape(rows, samples), *tables).reshape(lead + (2 * samples,))


def all_spectra(values, tables):
    rows = [math.prod(value.shape[:-1]) for value in values]
    samples = values[0].shape[-1]
    flat = split_dot(
        jnp.concatenate([value.reshape(-1, samples) for value in values]), *tables
    )
    starts = [sum(rows[:index]) for index in range(len(rows))]
    return [
        flat[start : start + count].reshape(value.shape[:-1] + (2 * samples,))
        for start, count, value in zip(starts, rows, values)
    ]


def with_sums(values):
    half = values.shape[-1] // 2
    total = values[..., :half] + values[..., half:]
    return jnp.concatenate([values, total], axis=-1)


def products(total_ref, lefts, right_ref):
    _, sources, width = total_ref.shape
    half = width // 2
    zero = jnp.zeros((sources, LANES), jnp.float32)
    for tile in range(half // LANES):
        real = pl.ds(tile * LANES, LANES)
        imag = pl.ds(half + tile * LANES, LANES)
        both = pl.ds(width + tile * LANES, LANES)
        for group in range(0, len(lefts), GROUP):
            members = lefts[group : group + GROUP]
            sums = [(zero, zero, zero) for _ in members]
            for bounce in range(right_ref.shape[0]):
                at = slice(bounce, bounce + 1)
                right_real = right_ref[bounce, :, real]
                right_imag = right_ref[bounce, :, imag]
                right_more = right_imag - right_real
                right_both = right_imag + right_real
                for index, (_, left_ref, row) in enumerate(members):
                    one, two, three = sums[index]
                    sums[index] = (
                        one + left_ref[row, at, both] * right_real,
                        two + left_ref[row, at, real] * right_more,
                        three + left_ref[row, at, imag] * right_both,
                    )
            for (one, two, three), (row, _, _) in zip(sums, members):
                total_ref[row, :, real] = one - three
                total_ref[row, :, imag] = one + two


def to_traces(prediction_ref, total_ref, tables):
    rows, sources, width = total_ref.shape
    flat = total_ref[...].reshape(rows * sources, width) * (2.0 / width)
    prediction_ref[...] = split_dot(flat, *tables, of=1).reshape(prediction_ref.shape)


def tap_rows(near, taps):
    inner = -(-near * taps // SUBLANES) * SUBLANES
    return inner, inner + -(-taps // SUBLANES) * SUBLANES


def lay_weights(weights_ref, scratch, filters_ref):
    near, receivers, sources, taps = filters_ref.shape
    inner, rows = tap_rows(near, taps)
    scratch[...] = jnp.zeros(scratch.shape, jnp.float32)
    lanes = receivers * sources
    for copy in range(LANES // lanes):
        for step in range(near):
            for row in range(receivers):
                receiver = row + 1 - step
                if 0 <= receiver < receivers:
                    at = pl.ds(copy * lanes + row * sources, sources)
                    scratch[at, step * taps : (step + 1) * taps] = filters_ref[step, receiver]
    for copy in range(LANES // (2 * sources)):
        for row, value in enumerate((filters_ref[0, 0], filters_ref[near - 1, receivers - 1])):
            at = pl.ds((copy * 2 + row) * sources, sources)
            scratch[at, inner : inner + taps] = value
    weights_ref[...] = scratch[...].T[:rows]


def turn(turned, prediction):
    receivers, sources, samples = prediction.shape
    lanes = receivers * sources
    per = samples * lanes // LANES
    zero = jnp.zeros((lanes, LANES), jnp.float32)
    for block in range(per // LANES + 2):
        side = []
        for start in range(0, samples, per):
            at = start + (block - 1) * LANES
            if 0 <= at < samples:
                side.append(prediction[:, :, at : at + LANES].reshape(lanes, LANES))
            else:
                side.append(zero)
        turned[pl.ds(block * LANES, LANES)] = jnp.concatenate(side, axis=0).T


def turn_back(value, receivers, sources):
    per = value.shape[0]
    parts = LANES // (receivers * sources)
    back = jnp.concatenate([value[at : at + LANES].T for at in range(0, per, LANES)], axis=1)
    back = back.reshape(parts, receivers, sources, per)
    return jnp.concatenate([back[part] for part in range(parts)], axis=2)


def matched(prediction, weights_ref, offsets_ref, turned, sums):
    receivers, sources, samples = prediction.shape
    near, taps = sums.shape[0], offsets_ref.shape[0]
    per = samples * receivers * sources // LANES
    turn(turned, prediction)
    chunk = min(per, CHUNK)
    for first in range(0, per, chunk):
        totals = [jnp.zeros((chunk, LANES), jnp.float32) for _ in range(near)]
        for tap in range(taps):
            shifted = turned[pl.ds(LANES + first - offsets_ref[tap], chunk), :]
            for step in range(near):
                at = step * taps + tap
                totals[step] = totals[step] + weights_ref[at : at + 1] * shifted
        for step in range(near):
            sums[step, pl.ds(first, chunk)] = totals[step]
    added = [None] * receivers
    for step in range(near):
        back = turn_back(sums[step, pl.ds(0, per)], receivers, sources)
        for row in range(receivers):
            receiver = row + 1 - step
            if 0 <= receiver < receivers:
                before = added[receiver]
                added[receiver] = back[row] if before is None else before + back[row]
    return added


def matched_halo(prediction, weights_ref, offsets_ref, turned):
    two, sources, samples = prediction.shape
    taps = offsets_ref.shape[0]
    first_tap = weights_ref.shape[0] - -(-taps // SUBLANES) * SUBLANES
    per = samples * two * sources // LANES
    turn(turned, prediction)
    total = jnp.zeros((per, LANES), jnp.float32)
    for tap in range(taps):
        shifted = turned[pl.ds(LANES - offsets_ref[tap], per), :]
        total = total + weights_ref[first_tap + tap : first_tap + tap + 1] * shifted
    return turn_back(total, two, sources)


def first_kernel(
    phases_ref, filters_ref, here_ref, right_ref,
    high_ref, low_ref, weights_ref, here_out, right_out, turned,
):
    dft_tables(high_ref, low_ref, phases_ref)
    lay_weights(weights_ref, turned, filters_ref)
    here, right = all_spectra(
        [here_ref[...], right_ref[...]], (high_ref[...], low_ref[...])
    )
    here_out[...] = with_sums(here)
    right_out[...] = right


def second_kernel(high_ref, low_ref, one_ref, *refs):
    right_refs, (one_out, right_out) = refs[:-2], refs[-2:]
    one, *right = all_spectra(
        [one_ref[...]] + [ref[...] for ref in right_refs], (high_ref[...], low_ref[...])
    )
    one_out[...] = with_sums(one)
    held = right_refs[0].shape[0]
    for block, value in enumerate(right):
        right_out[pl.ds(block * held, held)] = value


def position(slots, blocks):
    row, column = lax.axis_index("rcv"), lax.axis_index("src")
    return row, column, row // blocks == column // slots


def place_of(column, slot, slots, held):
    first = jnp.bitwise_xor(column, slot) % slots * held
    return pl.ds(pl.multiple_of(first, held), held)


def edge_kernel(slots, blocks, *refs):
    near_ref, far_ref = refs[3 * slots :]
    row, column, same = position(slots, blocks)
    odd = row % 2 == 1
    receivers, held, _ = refs[0].shape
    for slot in range(slots):
        these = place_of(column, slot, slots, held)
        here, one, two = refs[3 * slot : 3 * slot + 3]
        for index, (yes, no) in enumerate(((here, one), (one, two))):
            first = jnp.where(same, yes[0], no[0])
            last = jnp.where(same, yes[receivers - 1], no[receivers - 1])
            near_ref[index, these] = jnp.where(odd, first, last)
            far_ref[index, these] = jnp.where(odd, last, first)


def main_kernel(
    slots, blocks, offsets_from, high_ref, low_ref, weights_ref, right_a, right_b, one_ref, *refs
):
    columns, refs = refs[: 2 * slots - 1], refs[2 * slots - 1 :]
    right_refs, refs = refs[:-9], refs[-9:]
    out_ref, right_ref, total, prediction, turned, sums, offsets_ref, arrived, left_ref = refs
    copy = pltpu.make_async_copy(offsets_from, offsets_ref, arrived)
    copy.start()
    row, column, same = position(slots, blocks)
    count = right_a.shape[0]
    traces = [columns[0][...]]
    for slot in range(1, slots):
        one, two = columns[2 * slot - 1 : 2 * slot + 1]
        traces.append(jnp.where(same, one[...], two[...]))
    spectra_of = all_spectra(
        traces + [ref[...] for ref in right_refs], (high_ref[...], low_ref[...])
    )
    place = 0
    for value in [right_a, right_b] + spectra_of[slots:]:
        step = min(count, value.shape[0])
        for first in range(0, value.shape[0], step):
            at = jnp.bitwise_xor(row, place // count) % blocks * count + place % count
            right_ref[pl.ds(at, step)] = value[first : first + step]
            place += step
    receivers, held, _ = one_ref.shape
    for slot in range(slots):
        these = place_of(column, slot, slots, held)
        mirror = with_sums(spectra_of[slot])
        if slot == 0:
            mirror = jnp.where(same, one_ref[...], mirror)
        for receiver in range(receivers):
            left_ref[receiver, these] = mirror[receiver]
    products(total, [(row, left_ref, row) for row in range(receivers)], right_ref)
    to_traces(prediction, total, (high_ref[...], low_ref[...]))
    copy.wait()
    added = matched(prediction, weights_ref, offsets_ref, turned, sums)
    for receiver in range(receivers):
        out_ref[receiver] = added[receiver]


def mirror_kernel(
    blocks, offsets_from, high_ref, low_ref, weights_ref, near_ref, far_ref, part_ref,
    right_ref, out_ref, halo_ref, total, prediction, turned, offsets_ref, arrived, outer,
):
    copy = pltpu.make_async_copy(offsets_from, offsets_ref, arrived)
    copy.start()
    row = lax.axis_index("rcv")
    odd, lower = row % 2 == 1, row < blocks
    before = jnp.where(odd, near_ref[...], far_ref[...])
    after = jnp.where(odd, far_ref[...], near_ref[...])
    zero = jnp.zeros(before.shape[1:], jnp.float32)
    for which, (value, end, none) in enumerate(
        (
            (before, row % blocks == 0, lower),
            (after, row % blocks == blocks - 1, jnp.logical_not(lower)),
        )
    ):
        own, mirror = value[0], value[1]
        outer[which] = jnp.where(end, jnp.where(none, zero, mirror), own)
        outer[2 + which] = jnp.where(end, jnp.where(none, own, zero), mirror)
    tables = (high_ref[...], low_ref[...])
    halo_ref[...] = with_sums(spectra(outer, tables))
    products(total, [(0, halo_ref, 2), (1, halo_ref, 3)], right_ref)
    to_traces(prediction, total, tables)
    copy.wait()
    added = matched_halo(prediction[...], weights_ref, offsets_ref, turned)
    last = out_ref.shape[0] - 1
    out_ref[...] = part_ref[...]
    out_ref[0] = out_ref[0] + added[0]
    out_ref[last] = out_ref[last] + added[1]


def own_kernel(
    slots, blocks, offsets_from, high_ref, low_ref, weights_ref, right_ref, halo_ref,
    recorded_ref, here_ref, one_ref, *refs
):
    columns, refs = refs[: 2 * slots - 2], refs[2 * slots - 2 :]
    out_ref, total, prediction, turned, sums, offsets_ref, arrived, left_ref = refs
    copy = pltpu.make_async_copy(offsets_from, offsets_ref, arrived)
    copy.start()
    tables = (high_ref[...], low_ref[...])
    row, column, same = position(slots, blocks)
    receivers, held, _ = here_ref.shape
    for slot in range(slots):
        these = place_of(column, slot, slots, held)
        if slot == 0:
            own = jnp.where(same, here_ref[...], one_ref[...])
        else:
            here, one = columns[2 * slot - 2 : 2 * slot]
            chosen = jnp.where(same, here[...], one[...])
            own = with_sums(all_spectra([chosen], tables)[0])
        for receiver in range(receivers):
            left_ref[receiver, these] = own[receiver]
    lefts = [(row, left_ref, row) for row in range(receivers)]
    lefts += [(receivers, halo_ref, 0), (receivers + 1, halo_ref, 1)]
    products(total, lefts, right_ref)
    to_traces(prediction, total, tables)
    copy.wait()
    last = receivers - 1
    added = matched(prediction[:receivers], weights_ref, offsets_ref, turned, sums)
    outer = matched_halo(prediction[receivers:], weights_ref, offsets_ref, turned)
    for receiver in range(receivers):
        value = recorded_ref[receiver] - added[receiver]
        if receiver == 0:
            value = value - outer[0]
        if receiver == last:
            value = value - outer[1]
        out_ref[receiver] = value


def last_kernel(part_ref, arrived_ref, out_ref):
    out_ref[...] = part_ref[...] - arrived_ref[...]


def call(kernel, arrays, outs, scratch, in_place=0):
    shapes = [s if hasattr(s, "dtype") else jax.ShapeDtypeStruct(s, jnp.float32) for s in outs]
    vmem = pl.BlockSpec(memory_space=pltpu.VMEM)
    return pl.pallas_call(
        kernel,
        out_shape=shapes,
        in_specs=[pl.BlockSpec(memory_space=pl.ANY)] * in_place + [vmem] * (len(arrays) - in_place),
        out_specs=[vmem] * len(shapes),
        scratch_shapes=[
            s if not isinstance(s, tuple) else pltpu.VMEM(s, jnp.float32) for s in scratch
        ],
        compiler_params=pltpu.CompilerParams(vmem_limit_bytes=VMEM_LIMIT),
    )(*arrays)


def local(rows, columns, rb_data, bs_data, recorded, filters, offsets):
    receivers, left_count, samples = rb_data.shape
    right_count, sources, _ = bs_data.shape
    near_count, taps = filters.shape[:2]
    slots, blocks = columns // 2, rows // 2
    def permute(array, target):
        pairs = []
        for i in range(rows):
            for j in range(columns):
                to = target(i, j)
                if to is not None:
                    pairs.append((i * columns + j, to[0] * columns + to[1]))
        return lax.ppermute(array, AXES, pairs)

    def is_same(i, j):
        return i // blocks == j // slots

    cut = 2 * blocks // 3 + 1
    width = 2 * samples
    held = slots * left_count
    one = permute(
        rb_data, lambda i, j: (i, j ^ slots) if is_same(i, j) else (i ^ blocks, j)
    )
    some = [permute(bs_data, lambda i, j, k=k: (i ^ k, j)) for k in range(1, cut)]
    heres = [rb_data] + [
        permute(rb_data, lambda i, j, k=k: (i, j ^ k)) for k in range(1, slots)
    ]
    table = jax.ShapeDtypeStruct((samples, width), jnp.bfloat16)
    left_shape = (receivers, left_count, width + samples)
    high, low, weights, here_spectra, right_a = call(
        first_kernel,
        [jnp.asarray(phases(samples)), filters.transpose(0, 2, 3, 1), rb_data, bs_data],
        [
            table, table, (tap_rows(near_count, taps)[1], LANES), left_shape,
            (right_count, sources, width),
        ],
        [(LANES, LANES)],
    )
    one, some, heres, high, low, weights, here_spectra, right_a = lax.optimization_barrier(
        (one, some, heres, high, low, weights, here_spectra, right_a)
    )
    two = permute(one, lambda i, j: (i, j ^ slots) if is_same(i, j) else None)
    ones = [permute(one, lambda i, j, k=k: (i, j ^ k)) for k in range(1, slots)]
    rest = []
    for k in range(cut, blocks):
        bits = [1 << n for n in range(blocks) if 0 < k ^ (1 << n) < cut][:2]
        part = right_count // len(bits)
        for n, bit in enumerate(bits):
            of = some[(k ^ bit) - 1][n * part : (n + 1) * part if n + 1 < len(bits) else None]
            rest.append(permute(of, lambda i, j, bit=bit: (i ^ bit, j)))
    mirror_weights = permute(weights, lambda i, j: (i ^ blocks, j))
    one_spectra, right_b = call(
        second_kernel, [high, low, one] + some,
        [left_shape, (len(some) * right_count, sources, width)], [],
    )
    two, ones, mirror_weights, one_spectra, right_b = lax.optimization_barrier(
        (two, ones, mirror_weights, one_spectra, right_b)
    )
    gathered = [two]
    for k in range(1, slots):
        gathered += [heres[k], ones[k - 1]]
        gathered.append(permute(two, lambda i, j, k=k: None if is_same(i, j) else (i, j ^ k)))
    gathered, rest = lax.optimization_barrier((gathered, rest))
    edge_shape = (2, held, samples)
    near, far = call(
        functools.partial(edge_kernel, slots, blocks), [rb_data, one] + gathered,
        [edge_shape, edge_shape], [],
    )

    def in_half(i, at):
        return at % blocks + i // blocks * blocks

    near = permute(near, lambda i, j: (i ^ 1, j))
    far = permute(far, lambda i, j: (in_half(i, i + 1 if i % 2 else i - 1), j))
    per = samples * receivers * sources // LANES
    right_shape = (blocks * right_count, sources, width)
    own_shape = (receivers, held, width + samples)

    def scratch_of(predicted):
        return [(predicted, sources, width), (predicted, sources, samples), (per + 2 * LANES, LANES)]

    sums = [(near_count, per, LANES)]
    taken = [pltpu.SMEM(offsets.shape, jnp.int32), pltpu.SemaphoreType.DMA(())]
    ones_twos = [two]
    heres_ones = []
    for k in range(1, slots):
        ones_twos += gathered[3 * k - 1 : 3 * k + 1]
        heres_ones += gathered[3 * k - 2 : 3 * k]
    part, right = call(
        functools.partial(main_kernel, slots, blocks),
        [offsets, high, low, mirror_weights, right_a, right_b, one_spectra] + ones_twos + rest,
        [recorded.shape, right_shape],
        scratch_of(receivers) + sums + taken + [own_shape],
        in_place=1,
    )
    mirror_part, halo = call(
        functools.partial(mirror_kernel, blocks),
        [offsets, high, low, mirror_weights, near, far, part, right],
        [recorded.shape, (4, held, width + samples)],
        scratch_of(2) + taken + [(4, held, samples)],
        in_place=1,
    )
    arrived = permute(mirror_part, lambda i, j: (i ^ blocks, j))
    (own_part,) = call(
        functools.partial(own_kernel, slots, blocks),
        [offsets, high, low, weights, right, halo, recorded, here_spectra, one_spectra]
        + heres_ones,
        [recorded.shape],
        scratch_of(receivers + 2) + sums + taken + [own_shape],
        in_place=1,
    )
    (out,) = call(last_kernel, [own_part, arrived], [recorded.shape], [])
    return out


def solution(mesh):
    in_specs = (
        P("rcv", "src", None),
        P("rcv", "src", None),
        P("rcv", "src", None),
        P(None, None, "rcv", "src"),
        P(),
    )
    out_specs = P("rcv", "src", None)
    body = functools.partial(local, mesh.shape["rcv"], mesh.shape["src"])
    return jax.shard_map(body, mesh=mesh, in_specs=in_specs, out_specs=out_specs, check_vma=False)
```

```python
import functools
import math

import jax
import jax.numpy as jnp
import numpy as np
from jax import lax
from jax.experimental import pallas as pl
from jax.experimental.pallas import tpu as pltpu
from jax.sharding import PartitionSpec as P

LANES = 128
SUBLANES = 8
VMEM_LIMIT = 20 * 1024 * 1024
AXES = ("rcv", "src")
STEP = 32
GROUP = 6
CHUNK = 64


def phases(samples):
    fine = np.arange(STEP, dtype=np.int64)
    coarse = np.arange(0, samples, STEP, dtype=np.int64)
    times = np.concatenate([coarse, fine])[:, None]
    odd = 2 * np.arange(samples, dtype=np.int64)[None, :] + 1
    phase = (times * odd % (4 * samples)).astype(np.float64) * (math.pi / (2 * samples))
    return np.concatenate([np.cos(phase), np.sin(phase)], axis=0).astype(np.float32)


def dft_tables(high_ref, low_ref, phases_ref):
    samples = high_ref.shape[0]
    coarse = samples // STEP
    half = phases_ref.shape[0] // 2
    cos_fine = phases_ref[coarse:half]
    sin_fine = phases_ref[half + coarse :]
    for step in range(coarse):
        cos_step = phases_ref[step : step + 1]
        sin_step = phases_ref[half + step : half + step + 1]
        cosine = cos_step * cos_fine - sin_step * sin_fine
        sine = sin_step * cos_fine + cos_step * sin_fine
        for value, at in ((cosine, 0), (-sine, samples)):
            high = value.astype(jnp.bfloat16)
            where = (pl.ds(step * STEP, STEP), pl.ds(at, samples))
            high_ref[where] = high
            low_ref[where] = (value - high.astype(jnp.float32)).astype(jnp.bfloat16)


def split_dot(rows, high_table, low_table, of=0):
    high = rows.astype(jnp.bfloat16)
    low = (rows - high.astype(jnp.float32)).astype(jnp.bfloat16)

    def dot(left, right):
        return lax.dot_general(
            left, right, (((1,), (of,)), ((), ())), preferred_element_type=jnp.float32
        )

    return dot(high, high_table) + (dot(low, high_table) + dot(high, low_table))


def spectra(traces_ref, tables):
    lead = traces_ref.shape[:-1]
    samples = traces_ref.shape[-1]
    rows = math.prod(lead)
    return split_dot(traces_ref[...].reshape(rows, samples), *tables).reshape(lead + (2 * samples,))


def all_spectra(values, tables):
    rows = [math.prod(value.shape[:-1]) for value in values]
    samples = values[0].shape[-1]
    flat = split_dot(
        jnp.concatenate([value.reshape(-1, samples) for value in values]), *tables
    )
    starts = [sum(rows[:index]) for index in range(len(rows))]
    return [
        flat[start : start + count].reshape(value.shape[:-1] + (2 * samples,))
        for start, count, value in zip(starts, rows, values)
    ]


def with_sums(values):
    half = values.shape[-1] // 2
    total = values[..., :half] + values[..., half:]
    return jnp.concatenate([values, total], axis=-1)


def products(total_ref, lefts, right_ref):
    _, sources, width = total_ref.shape
    half = width // 2
    zero = jnp.zeros((sources, LANES), jnp.float32)
    for tile in range(half // LANES):
        real = pl.ds(tile * LANES, LANES)
        imag = pl.ds(half + tile * LANES, LANES)
        both = pl.ds(width + tile * LANES, LANES)
        for group in range(0, len(lefts), GROUP):
            members = lefts[group : group + GROUP]
            sums = [(zero, zero, zero) for _ in members]
            for bounce in range(right_ref.shape[0]):
                at = slice(bounce, bounce + 1)
                right_real = right_ref[bounce, :, real]
                right_imag = right_ref[bounce, :, imag]
                right_more = right_imag - right_real
                right_both = right_imag + right_real
                for index, (_, left_ref, row) in enumerate(members):
                    one, two, three = sums[index]
                    sums[index] = (
                        one + left_ref[row, at, both] * right_real,
                        two + left_ref[row, at, real] * right_more,
                        three + left_ref[row, at, imag] * right_both,
                    )
            for (one, two, three), (row, _, _) in zip(sums, members):
                total_ref[row, :, real] = one - three
                total_ref[row, :, imag] = one + two


def to_traces(prediction_ref, total_ref, tables):
    rows, sources, width = total_ref.shape
    flat = total_ref[...].reshape(rows * sources, width) * (2.0 / width)
    prediction_ref[...] = split_dot(flat, *tables, of=1).reshape(prediction_ref.shape)


def tap_rows(near, taps):
    inner = -(-near * taps // SUBLANES) * SUBLANES
    return inner, inner + -(-taps // SUBLANES) * SUBLANES


def lay_weights(weights_ref, scratch, filters_ref):
    near, receivers, sources, taps = filters_ref.shape
    inner, rows = tap_rows(near, taps)
    scratch[...] = jnp.zeros(scratch.shape, jnp.float32)
    lanes = receivers * sources
    for copy in range(LANES // lanes):
        for step in range(near):
            for row in range(receivers):
                receiver = row + 1 - step
                if 0 <= receiver < receivers:
                    at = pl.ds(copy * lanes + row * sources, sources)
                    scratch[at, step * taps : (step + 1) * taps] = filters_ref[step, receiver]
    for copy in range(LANES // (2 * sources)):
        for row, value in enumerate((filters_ref[0, 0], filters_ref[near - 1, receivers - 1])):
            at = pl.ds((copy * 2 + row) * sources, sources)
            scratch[at, inner : inner + taps] = value
    weights_ref[...] = scratch[...].T[:rows]


def turn(turned, prediction):
    receivers, sources, samples = prediction.shape
    lanes = receivers * sources
    per = samples * lanes // LANES
    zero = jnp.zeros((lanes, LANES), jnp.float32)
    for block in range(per // LANES + 2):
        side = []
        for start in range(0, samples, per):
            at = start + (block - 1) * LANES
            if 0 <= at < samples:
                side.append(prediction[:, :, at : at + LANES].reshape(lanes, LANES))
            else:
                side.append(zero)
        turned[pl.ds(block * LANES, LANES)] = jnp.concatenate(side, axis=0).T


def turn_back(value, receivers, sources):
    per = value.shape[0]
    parts = LANES // (receivers * sources)
    back = jnp.concatenate([value[at : at + LANES].T for at in range(0, per, LANES)], axis=1)
    back = back.reshape(parts, receivers, sources, per)
    return jnp.concatenate([back[part] for part in range(parts)], axis=2)


def matched(prediction, weights_ref, offsets_ref, turned, sums):
    receivers, sources, samples = prediction.shape
    near, taps = sums.shape[0], offsets_ref.shape[0]
    per = samples * receivers * sources // LANES
    turn(turned, prediction)
    chunk = min(per, CHUNK)
    for first in range(0, per, chunk):
        totals = [jnp.zeros((chunk, LANES), jnp.float32) for _ in range(near)]
        for tap in range(taps):
            shifted = turned[pl.ds(LANES + first - offsets_ref[tap], chunk), :]
            for step in range(near):
                at = step * taps + tap
                totals[step] = totals[step] + weights_ref[at : at + 1] * shifted
        for step in range(near):
            sums[step, pl.ds(first, chunk)] = totals[step]
    added = [None] * receivers
    for step in range(near):
        back = turn_back(sums[step, pl.ds(0, per)], receivers, sources)
        for row in range(receivers):
            receiver = row + 1 - step
            if 0 <= receiver < receivers:
                before = added[receiver]
                added[receiver] = back[row] if before is None else before + back[row]
    return added


def matched_halo(prediction, weights_ref, offsets_ref, turned):
    two, sources, samples = prediction.shape
    taps = offsets_ref.shape[0]
    first_tap = weights_ref.shape[0] - -(-taps // SUBLANES) * SUBLANES
    per = samples * two * sources // LANES
    turn(turned, prediction)
    total = jnp.zeros((per, LANES), jnp.float32)
    for tap in range(taps):
        shifted = turned[pl.ds(LANES - offsets_ref[tap], per), :]
        total = total + weights_ref[first_tap + tap : first_tap + tap + 1] * shifted
    return turn_back(total, two, sources)


def first_kernel(
    phases_ref, filters_ref, here_ref, right_ref,
    high_ref, low_ref, weights_ref, here_out, right_out, turned,
):
    dft_tables(high_ref, low_ref, phases_ref)
    lay_weights(weights_ref, turned, filters_ref)
    here, right = all_spectra(
        [here_ref[...], right_ref[...]], (high_ref[...], low_ref[...])
    )
    here_out[...] = with_sums(here)
    right_out[...] = right


def second_kernel(high_ref, low_ref, one_ref, *refs):
    right_refs, (one_out, right_out) = refs[:-2], refs[-2:]
    one, *right = all_spectra(
        [one_ref[...]] + [ref[...] for ref in right_refs], (high_ref[...], low_ref[...])
    )
    one_out[...] = with_sums(one)
    held = right_refs[0].shape[0]
    for block, value in enumerate(right):
        right_out[pl.ds(block * held, held)] = value


def position(slots, blocks):
    row, column = lax.axis_index("rcv"), lax.axis_index("src")
    return row, column, row // blocks == column // slots


def place_of(column, slot, slots, held):
    first = jnp.bitwise_xor(column, slot) % slots * held
    return pl.ds(pl.multiple_of(first, held), held)


def edge_kernel(slots, blocks, *refs):
    near_ref, far_ref = refs[3 * slots :]
    row, column, same = position(slots, blocks)
    odd = row % 2 == 1
    receivers, held, _ = refs[0].shape
    for slot in range(slots):
        these = place_of(column, slot, slots, held)
        here, one, two = refs[3 * slot : 3 * slot + 3]
        for index, (yes, no) in enumerate(((here, one), (one, two))):
            first = jnp.where(same, yes[0], no[0])
            last = jnp.where(same, yes[receivers - 1], no[receivers - 1])
            near_ref[index, these] = jnp.where(odd, first, last)
            far_ref[index, these] = jnp.where(odd, last, first)


def main_kernel(
    slots, blocks, offsets_from, high_ref, low_ref, weights_ref, right_a, right_b, one_ref, *refs
):
    columns, refs = refs[: 2 * slots - 1], refs[2 * slots - 1 :]
    right_refs, refs = refs[:-10], refs[-10:]
    ends_ref, out_ref, right_ref, total, prediction, turned, sums, offsets_ref, arrived = refs[:9]
    left_ref = refs[9]
    copy = pltpu.make_async_copy(offsets_from, offsets_ref, arrived)
    copy.start()
    row, column, same = position(slots, blocks)
    count = right_a.shape[0]
    traces = [columns[0][...]]
    for slot in range(1, slots):
        one, two = columns[2 * slot - 1 : 2 * slot + 1]
        traces.append(jnp.where(same, one[...], two[...]))
    spectra_of = all_spectra(
        traces + [ref[...] for ref in right_refs], (high_ref[...], low_ref[...])
    )
    place = 0
    for value in [right_a, right_b] + spectra_of[slots:]:
        step = min(count, value.shape[0])
        for first in range(0, value.shape[0], step):
            at = jnp.bitwise_xor(row, place // count) % blocks * count + place % count
            right_ref[pl.ds(at, step)] = value[first : first + step]
            place += step
    receivers, held, _ = one_ref.shape
    for slot in range(slots):
        these = place_of(column, slot, slots, held)
        mirror = with_sums(spectra_of[slot])
        if slot == 0:
            mirror = jnp.where(same, one_ref[...], mirror)
        for receiver in range(receivers):
            left_ref[receiver, these] = mirror[receiver]
    products(total, [(row, left_ref, row) for row in range(receivers)], right_ref)
    to_traces(prediction, total, (high_ref[...], low_ref[...]))
    copy.wait()
    added = matched(prediction, weights_ref, offsets_ref, turned, sums)
    ends_ref[0] = added[0]
    ends_ref[1] = added[-1]
    for receiver in range(1, receivers - 1):
        out_ref[receiver - 1] = added[receiver]


def mirror_kernel(
    blocks, offsets_from, high_ref, low_ref, weights_ref, near_ref, far_ref, part_ref,
    right_ref, out_ref, halo_ref, total, prediction, turned, offsets_ref, arrived, outer,
):
    copy = pltpu.make_async_copy(offsets_from, offsets_ref, arrived)
    copy.start()
    row = lax.axis_index("rcv")
    odd, lower = row % 2 == 1, row < blocks
    before = jnp.where(odd, near_ref[...], far_ref[...])
    after = jnp.where(odd, far_ref[...], near_ref[...])
    zero = jnp.zeros(before.shape[1:], jnp.float32)
    for which, (value, end, none) in enumerate(
        (
            (before, row % blocks == 0, lower),
            (after, row % blocks == blocks - 1, jnp.logical_not(lower)),
        )
    ):
        own, mirror = value[0], value[1]
        outer[which] = jnp.where(end, jnp.where(none, zero, mirror), own)
        outer[2 + which] = jnp.where(end, jnp.where(none, own, zero), mirror)
    tables = (high_ref[...], low_ref[...])
    halo_ref[...] = with_sums(spectra(outer, tables))
    products(total, [(0, halo_ref, 2), (1, halo_ref, 3)], right_ref)
    to_traces(prediction, total, tables)
    copy.wait()
    added = matched_halo(prediction[...], weights_ref, offsets_ref, turned)
    out_ref[...] = part_ref[...] + added


def own_kernel(
    slots, blocks, offsets_from, high_ref, low_ref, weights_ref, right_ref, halo_ref,
    recorded_ref, inner_ref, here_ref, one_ref, *refs
):
    columns, refs = refs[: 2 * slots - 2], refs[2 * slots - 2 :]
    out_ref, total, prediction, turned, sums, offsets_ref, arrived, left_ref = refs
    copy = pltpu.make_async_copy(offsets_from, offsets_ref, arrived)
    copy.start()
    tables = (high_ref[...], low_ref[...])
    row, column, same = position(slots, blocks)
    receivers, held, _ = here_ref.shape
    for slot in range(slots):
        these = place_of(column, slot, slots, held)
        if slot == 0:
            own = jnp.where(same, here_ref[...], one_ref[...])
        else:
            here, one = columns[2 * slot - 2 : 2 * slot]
            chosen = jnp.where(same, here[...], one[...])
            own = with_sums(all_spectra([chosen], tables)[0])
        for receiver in range(receivers):
            left_ref[receiver, these] = own[receiver]
    lefts = [(row, left_ref, row) for row in range(receivers)]
    lefts += [(receivers, halo_ref, 0), (receivers + 1, halo_ref, 1)]
    products(total, lefts, right_ref)
    to_traces(prediction, total, tables)
    copy.wait()
    last = receivers - 1
    added = matched(prediction[:receivers], weights_ref, offsets_ref, turned, sums)
    outer = matched_halo(prediction[receivers:], weights_ref, offsets_ref, turned)
    for receiver in range(receivers):
        value = recorded_ref[receiver] - added[receiver]
        if receiver == 0:
            value = value - outer[0]
        if receiver == last:
            value = value - outer[1]
        if 0 < receiver < last:
            value = value - inner_ref[receiver - 1]
        out_ref[receiver] = value


def last_kernel(part_ref, ends_ref, out_ref):
    last = out_ref.shape[0] - 1
    out_ref[...] = part_ref[...]
    out_ref[0] = part_ref[0] - ends_ref[0]
    out_ref[last] = part_ref[last] - ends_ref[1]


def call(kernel, arrays, outs, scratch, in_place=0):
    shapes = [s if hasattr(s, "dtype") else jax.ShapeDtypeStruct(s, jnp.float32) for s in outs]
    vmem = pl.BlockSpec(memory_space=pltpu.VMEM)
    return pl.pallas_call(
        kernel,
        out_shape=shapes,
        in_specs=[pl.BlockSpec(memory_space=pl.ANY)] * in_place + [vmem] * (len(arrays) - in_place),
        out_specs=[vmem] * len(shapes),
        scratch_shapes=[
            s if not isinstance(s, tuple) else pltpu.VMEM(s, jnp.float32) for s in scratch
        ],
        compiler_params=pltpu.CompilerParams(vmem_limit_bytes=VMEM_LIMIT),
    )(*arrays)


def local(rows, columns, rb_data, bs_data, recorded, filters, offsets):
    receivers, left_count, samples = rb_data.shape
    right_count, sources, _ = bs_data.shape
    near_count, taps = filters.shape[:2]
    slots, blocks = columns // 2, rows // 2
    def permute(array, target):
        pairs = []
        for i in range(rows):
            for j in range(columns):
                to = target(i, j)
                if to is not None:
                    pairs.append((i * columns + j, to[0] * columns + to[1]))
        return lax.ppermute(array, AXES, pairs)

    def is_same(i, j):
        return i // blocks == j // slots

    cut = 2 * blocks // 3 + 1
    width = 2 * samples
    held = slots * left_count
    one = permute(
        rb_data, lambda i, j: (i, j ^ slots) if is_same(i, j) else (i ^ blocks, j)
    )
    some = [permute(bs_data, lambda i, j, k=k: (i ^ k, j)) for k in range(1, cut)]
    heres = [rb_data] + [
        permute(rb_data, lambda i, j, k=k: (i, j ^ k)) for k in range(1, slots)
    ]
    table = jax.ShapeDtypeStruct((samples, width), jnp.bfloat16)
    left_shape = (receivers, left_count, width + samples)
    high, low, weights, here_spectra, right_a = call(
        first_kernel,
        [jnp.asarray(phases(samples)), filters.transpose(0, 2, 3, 1), rb_data, bs_data],
        [
            table, table, (tap_rows(near_count, taps)[1], LANES), left_shape,
            (right_count, sources, width),
        ],
        [(LANES, LANES)],
    )
    one, some, heres, high, low, weights, here_spectra, right_a = lax.optimization_barrier(
        (one, some, heres, high, low, weights, here_spectra, right_a)
    )
    two = permute(one, lambda i, j: (i, j ^ slots) if is_same(i, j) else None)
    ones = [permute(one, lambda i, j, k=k: (i, j ^ k)) for k in range(1, slots)]
    rest = []
    for k in range(cut, blocks):
        bits = [1 << n for n in range(blocks) if 0 < k ^ (1 << n) < cut][:2]
        part = right_count // len(bits)
        for n, bit in enumerate(bits):
            of = some[(k ^ bit) - 1][n * part : (n + 1) * part if n + 1 < len(bits) else None]
            rest.append(permute(of, lambda i, j, bit=bit: (i ^ bit, j)))
    mirror_weights = permute(weights, lambda i, j: (i ^ blocks, j))
    one_spectra, right_b = call(
        second_kernel, [high, low, one] + some,
        [left_shape, (len(some) * right_count, sources, width)], [],
    )
    two, ones, mirror_weights, one_spectra, right_b = lax.optimization_barrier(
        (two, ones, mirror_weights, one_spectra, right_b)
    )
    gathered = [two]
    for k in range(1, slots):
        gathered += [heres[k], ones[k - 1]]
        gathered.append(permute(two, lambda i, j, k=k: None if is_same(i, j) else (i, j ^ k)))
    gathered, rest = lax.optimization_barrier((gathered, rest))
    edge_shape = (2, held, samples)
    near, far = call(
        functools.partial(edge_kernel, slots, blocks), [rb_data, one] + gathered,
        [edge_shape, edge_shape], [],
    )

    def in_half(i, at):
        return at % blocks + i // blocks * blocks

    near = permute(near, lambda i, j: (i ^ 1, j))
    far = permute(far, lambda i, j: (in_half(i, i + 1 if i % 2 else i - 1), j))
    per = samples * receivers * sources // LANES
    right_shape = (blocks * right_count, sources, width)
    own_shape = (receivers, held, width + samples)

    def scratch_of(predicted):
        return [(predicted, sources, width), (predicted, sources, samples), (per + 2 * LANES, LANES)]

    sums = [(near_count, per, LANES)]
    taken = [pltpu.SMEM(offsets.shape, jnp.int32), pltpu.SemaphoreType.DMA(())]
    ones_twos = [two]
    heres_ones = []
    for k in range(1, slots):
        ones_twos += gathered[3 * k - 1 : 3 * k + 1]
        heres_ones += gathered[3 * k - 2 : 3 * k]
    ends_shape = (2, sources, samples)
    ends, inner, right = call(
        functools.partial(main_kernel, slots, blocks),
        [offsets, high, low, mirror_weights, right_a, right_b, one_spectra] + ones_twos + rest,
        [ends_shape, (receivers - 2, sources, samples), right_shape],
        scratch_of(receivers) + sums + taken + [own_shape],
        in_place=1,
    )
    inner = permute(inner, lambda i, j: (i ^ blocks, j))
    ends, halo = call(
        functools.partial(mirror_kernel, blocks),
        [offsets, high, low, mirror_weights, near, far, ends, right],
        [ends_shape, (4, held, width + samples)],
        scratch_of(2) + taken + [(4, held, samples)],
        in_place=1,
    )
    ends = permute(ends, lambda i, j: (i ^ blocks, j))
    (own_part,) = call(
        functools.partial(own_kernel, slots, blocks),
        [offsets, high, low, weights, right, halo, recorded, inner, here_spectra, one_spectra]
        + heres_ones,
        [recorded.shape],
        scratch_of(receivers + 2) + sums + taken + [own_shape],
        in_place=1,
    )
    (out,) = call(last_kernel, [own_part, ends], [recorded.shape], [])
    return out


def solution(mesh):
    in_specs = (
        P("rcv", "src", None),
        P("rcv", "src", None),
        P("rcv", "src", None),
        P(None, None, "rcv", "src"),
        P(),
    )
    out_specs = P("rcv", "src", None)
    body = functools.partial(local, mesh.shape["rcv"], mesh.shape["src"])
    return jax.shard_map(body, mesh=mesh, in_specs=in_specs, out_specs=out_specs, check_vma=False)
```

```python
import functools
import math

import jax
import jax.numpy as jnp
import numpy as np
from jax import lax
from jax.experimental import pallas as pl
from jax.experimental.pallas import tpu as pltpu
from jax.sharding import PartitionSpec as P

LANES = 128
SUBLANES = 8
VMEM_LIMIT = 20 * 1024 * 1024
AXES = ("rcv", "src")
STEP = 32
GROUP = 6
CHUNK = 64


def phases(samples):
    fine = np.arange(STEP, dtype=np.int64)
    coarse = np.arange(0, samples, STEP, dtype=np.int64)
    times = np.concatenate([coarse, fine])[:, None]
    odd = 2 * np.arange(samples, dtype=np.int64)[None, :] + 1
    phase = (times * odd % (4 * samples)).astype(np.float64) * (math.pi / (2 * samples))
    return np.concatenate([np.cos(phase), np.sin(phase)], axis=0).astype(np.float32)


def dft_tables(high_ref, low_ref, phases_ref):
    samples = high_ref.shape[0]
    coarse = samples // STEP
    half = phases_ref.shape[0] // 2
    cos_fine = phases_ref[coarse:half]
    sin_fine = phases_ref[half + coarse :]
    for step in range(coarse):
        cos_step = phases_ref[step : step + 1]
        sin_step = phases_ref[half + step : half + step + 1]
        cosine = cos_step * cos_fine - sin_step * sin_fine
        sine = sin_step * cos_fine + cos_step * sin_fine
        for value, at in ((cosine, 0), (-sine, samples)):
            high = value.astype(jnp.bfloat16)
            where = (pl.ds(step * STEP, STEP), pl.ds(at, samples))
            high_ref[where] = high
            low_ref[where] = (value - high.astype(jnp.float32)).astype(jnp.bfloat16)


def split_dot(rows, high_table, low_table, of=0):
    high = rows.astype(jnp.bfloat16)
    low = (rows - high.astype(jnp.float32)).astype(jnp.bfloat16)

    def dot(left, right):
        return lax.dot_general(
            left, right, (((1,), (of,)), ((), ())), preferred_element_type=jnp.float32
        )

    return dot(high, high_table) + (dot(low, high_table) + dot(high, low_table))


def spectra(traces_ref, tables):
    lead = traces_ref.shape[:-1]
    samples = traces_ref.shape[-1]
    rows = math.prod(lead)
    return split_dot(traces_ref[...].reshape(rows, samples), *tables).reshape(lead + (2 * samples,))


def all_spectra(values, tables):
    rows = [math.prod(value.shape[:-1]) for value in values]
    samples = values[0].shape[-1]
    flat = split_dot(
        jnp.concatenate([value.reshape(-1, samples) for value in values]), *tables
    )
    starts = [sum(rows[:index]) for index in range(len(rows))]
    return [
        flat[start : start + count].reshape(value.shape[:-1] + (2 * samples,))
        for start, count, value in zip(starts, rows, values)
    ]


def with_sums(values):
    half = values.shape[-1] // 2
    total = values[..., :half] + values[..., half:]
    return jnp.concatenate([values, total], axis=-1)


def with_differences(values):
    half = values.shape[-1] // 2
    real, imag = values[..., :half], values[..., half:]
    return jnp.concatenate([real, imag - real, imag + real], axis=-1)


def products(total_ref, lefts, right_ref):
    _, sources, width = total_ref.shape
    half = width // 2
    zero = jnp.zeros((sources, LANES), jnp.float32)
    for tile in range(half // LANES):
        real = pl.ds(tile * LANES, LANES)
        imag = pl.ds(half + tile * LANES, LANES)
        both = pl.ds(width + tile * LANES, LANES)
        for group in range(0, len(lefts), GROUP):
            members = lefts[group : group + GROUP]
            sums = [(zero, zero, zero) for _ in members]
            for bounce in range(right_ref.shape[0]):
                at = slice(bounce, bounce + 1)
                right_real = right_ref[bounce, :, real]
                right_more = right_ref[bounce, :, imag]
                right_both = right_ref[bounce, :, both]
                for index, (_, left_ref, row) in enumerate(members):
                    one, two, three = sums[index]
                    sums[index] = (
                        one + left_ref[row, at, both] * right_real,
                        two + left_ref[row, at, real] * right_more,
                        three + left_ref[row, at, imag] * right_both,
                    )
            for (one, two, three), (row, _, _) in zip(sums, members):
                total_ref[row, :, real] = one - three
                total_ref[row, :, imag] = one + two


def to_traces(prediction_ref, total_ref, tables):
    rows, sources, width = total_ref.shape
    flat = total_ref[...].reshape(rows * sources, width) * (2.0 / width)
    prediction_ref[...] = split_dot(flat, *tables, of=1).reshape(prediction_ref.shape)


def tap_rows(near, taps):
    inner = -(-near * taps // SUBLANES) * SUBLANES
    return inner, inner + -(-taps // SUBLANES) * SUBLANES


def lay_weights(weights_ref, scratch, filters_ref):
    near, receivers, sources, taps = filters_ref.shape
    inner, rows = tap_rows(near, taps)
    scratch[...] = jnp.zeros(scratch.shape, jnp.float32)
    lanes = receivers * sources
    for copy in range(LANES // lanes):
        for step in range(near):
            for row in range(receivers):
                receiver = row + 1 - step
                if 0 <= receiver < receivers:
                    at = pl.ds(copy * lanes + row * sources, sources)
                    scratch[at, step * taps : (step + 1) * taps] = filters_ref[step, receiver]
    for copy in range(LANES // (2 * sources)):
        for row, value in enumerate((filters_ref[0, 0], filters_ref[near - 1, receivers - 1])):
            at = pl.ds((copy * 2 + row) * sources, sources)
            scratch[at, inner : inner + taps] = value
    weights_ref[...] = scratch[...].T[:rows]


def turn(turned, prediction):
    receivers, sources, samples = prediction.shape
    lanes = receivers * sources
    per = samples * lanes // LANES
    zero = jnp.zeros((lanes, LANES), jnp.float32)
    for block in range(per // LANES + 2):
        side = []
        for start in range(0, samples, per):
            at = start + (block - 1) * LANES
            if 0 <= at < samples:
                side.append(prediction[:, :, at : at + LANES].reshape(lanes, LANES))
            else:
                side.append(zero)
        turned[pl.ds(block * LANES, LANES)] = jnp.concatenate(side, axis=0).T


def turn_back(value, receivers, sources):
    per = value.shape[0]
    parts = LANES // (receivers * sources)
    back = jnp.concatenate([value[at : at + LANES].T for at in range(0, per, LANES)], axis=1)
    back = back.reshape(parts, receivers, sources, per)
    return jnp.concatenate([back[part] for part in range(parts)], axis=2)


def matched(prediction, weights_ref, offsets_ref, turned, sums):
    receivers, sources, samples = prediction.shape
    near, taps = sums.shape[0], offsets_ref.shape[0]
    per = samples * receivers * sources // LANES
    turn(turned, prediction)
    chunk = min(per, CHUNK)
    for first in range(0, per, chunk):
        totals = [jnp.zeros((chunk, LANES), jnp.float32) for _ in range(near)]
        for tap in range(taps):
            shifted = turned[pl.ds(LANES + first - offsets_ref[tap], chunk), :]
            for step in range(near):
                at = step * taps + tap
                totals[step] = totals[step] + weights_ref[at : at + 1] * shifted
        for step in range(near):
            sums[step, pl.ds(first, chunk)] = totals[step]
    added = [None] * receivers
    for step in range(near):
        back = turn_back(sums[step, pl.ds(0, per)], receivers, sources)
        for row in range(receivers):
            receiver = row + 1 - step
            if 0 <= receiver < receivers:
                before = added[receiver]
                added[receiver] = back[row] if before is None else before + back[row]
    return added


def matched_halo(prediction, weights_ref, offsets_ref, turned):
    two, sources, samples = prediction.shape
    taps = offsets_ref.shape[0]
    first_tap = weights_ref.shape[0] - -(-taps // SUBLANES) * SUBLANES
    per = samples * two * sources // LANES
    turn(turned, prediction)
    total = jnp.zeros((per, LANES), jnp.float32)
    for tap in range(taps):
        shifted = turned[pl.ds(LANES - offsets_ref[tap], per), :]
        total = total + weights_ref[first_tap + tap : first_tap + tap + 1] * shifted
    return turn_back(total, two, sources)


def first_kernel(
    phases_ref, filters_ref, here_ref, right_ref,
    high_ref, low_ref, weights_ref, here_out, right_out, turned,
):
    dft_tables(high_ref, low_ref, phases_ref)
    lay_weights(weights_ref, turned, filters_ref)
    here, right = all_spectra(
        [here_ref[...], right_ref[...]], (high_ref[...], low_ref[...])
    )
    here_out[...] = with_sums(here)
    right_out[...] = right


def second_kernel(high_ref, low_ref, one_ref, *refs):
    right_refs, (one_out, right_out) = refs[:-2], refs[-2:]
    one, *right = all_spectra(
        [one_ref[...]] + [ref[...] for ref in right_refs], (high_ref[...], low_ref[...])
    )
    one_out[...] = with_sums(one)
    held = right_refs[0].shape[0]
    for block, value in enumerate(right):
        right_out[pl.ds(block * held, held)] = value


def position(slots, blocks):
    row, column = lax.axis_index("rcv"), lax.axis_index("src")
    return row, column, row // blocks == column // slots


def place_of(column, slot, slots, held):
    first = jnp.bitwise_xor(column, slot) % slots * held
    return pl.ds(pl.multiple_of(first, held), held)


def edge_kernel(slots, blocks, *refs):
    near_ref, far_ref = refs[3 * slots :]
    row, column, same = position(slots, blocks)
    odd = row % 2 == 1
    receivers, held, _ = refs[0].shape
    for slot in range(slots):
        these = place_of(column, slot, slots, held)
        here, one, two = refs[3 * slot : 3 * slot + 3]
        for index, (yes, no) in enumerate(((here, one), (one, two))):
            first = jnp.where(same, yes[0], no[0])
            last = jnp.where(same, yes[receivers - 1], no[receivers - 1])
            near_ref[index, these] = jnp.where(odd, first, last)
            far_ref[index, these] = jnp.where(odd, last, first)


def main_kernel(
    slots, blocks, offsets_from, high_ref, low_ref, weights_ref, right_a, right_b, one_ref, *refs
):
    columns, refs = refs[: 2 * slots - 1], refs[2 * slots - 1 :]
    right_refs, refs = refs[:-10], refs[-10:]
    ends_ref, out_ref, right_ref, total, prediction, turned, sums, offsets_ref, arrived = refs[:9]
    left_ref = refs[9]
    copy = pltpu.make_async_copy(offsets_from, offsets_ref, arrived)
    copy.start()
    row, column, same = position(slots, blocks)
    count = right_a.shape[0]
    traces = [columns[0][...]]
    for slot in range(1, slots):
        one, two = columns[2 * slot - 1 : 2 * slot + 1]
        traces.append(jnp.where(same, one[...], two[...]))
    spectra_of = all_spectra(
        traces + [ref[...] for ref in right_refs], (high_ref[...], low_ref[...])
    )
    place = 0
    for value in [right_a, right_b] + spectra_of[slots:]:
        step = min(count, value.shape[0])
        for first in range(0, value.shape[0], step):
            at = jnp.bitwise_xor(row, place // count) % blocks * count + place % count
            right_ref[pl.ds(at, step)] = with_differences(value[first : first + step])
            place += step
    receivers, held, _ = one_ref.shape
    for slot in range(slots):
        these = place_of(column, slot, slots, held)
        mirror = with_sums(spectra_of[slot])
        if slot == 0:
            mirror = jnp.where(same, one_ref[...], mirror)
        for receiver in range(receivers):
            left_ref[receiver, these] = mirror[receiver]
    products(total, [(row, left_ref, row) for row in range(receivers)], right_ref)
    to_traces(prediction, total, (high_ref[...], low_ref[...]))
    copy.wait()
    added = matched(prediction, weights_ref, offsets_ref, turned, sums)
    ends_ref[0] = added[0]
    ends_ref[1] = added[-1]
    for receiver in range(1, receivers - 1):
        out_ref[receiver - 1] = added[receiver]


def mirror_kernel(
    blocks, offsets_from, high_ref, low_ref, weights_ref, near_ref, far_ref, part_ref,
    right_ref, out_ref, halo_ref, total, prediction, turned, offsets_ref, arrived, outer,
):
    copy = pltpu.make_async_copy(offsets_from, offsets_ref, arrived)
    copy.start()
    row = lax.axis_index("rcv")
    odd, lower = row % 2 == 1, row < blocks
    before = jnp.where(odd, near_ref[...], far_ref[...])
    after = jnp.where(odd, far_ref[...], near_ref[...])
    zero = jnp.zeros(before.shape[1:], jnp.float32)
    for which, (value, end, none) in enumerate(
        (
            (before, row % blocks == 0, lower),
            (after, row % blocks == blocks - 1, jnp.logical_not(lower)),
        )
    ):
        own, mirror = value[0], value[1]
        outer[which] = jnp.where(end, jnp.where(none, zero, mirror), own)
        outer[2 + which] = jnp.where(end, jnp.where(none, own, zero), mirror)
    tables = (high_ref[...], low_ref[...])
    halo_ref[...] = with_sums(spectra(outer, tables))
    products(total, [(0, halo_ref, 2), (1, halo_ref, 3)], right_ref)
    to_traces(prediction, total, tables)
    copy.wait()
    added = matched_halo(prediction[...], weights_ref, offsets_ref, turned)
    out_ref[...] = part_ref[...] + added


def own_kernel(
    slots, blocks, offsets_from, high_ref, low_ref, weights_ref, right_ref, halo_ref,
    recorded_ref, inner_ref, here_ref, one_ref, *refs
):
    columns, refs = refs[: 2 * slots - 2], refs[2 * slots - 2 :]
    out_ref, total, prediction, turned, sums, offsets_ref, arrived, left_ref = refs
    copy = pltpu.make_async_copy(offsets_from, offsets_ref, arrived)
    copy.start()
    tables = (high_ref[...], low_ref[...])
    row, column, same = position(slots, blocks)
    receivers, held, _ = here_ref.shape
    for slot in range(slots):
        these = place_of(column, slot, slots, held)
        if slot == 0:
            own = jnp.where(same, here_ref[...], one_ref[...])
        else:
            here, one = columns[2 * slot - 2 : 2 * slot]
            chosen = jnp.where(same, here[...], one[...])
            own = with_sums(all_spectra([chosen], tables)[0])
        for receiver in range(receivers):
            left_ref[receiver, these] = own[receiver]
    lefts = [(row, left_ref, row) for row in range(receivers)]
    lefts += [(receivers, halo_ref, 0), (receivers + 1, halo_ref, 1)]
    products(total, lefts, right_ref)
    to_traces(prediction, total, tables)
    copy.wait()
    last = receivers - 1
    added = matched(prediction[:receivers], weights_ref, offsets_ref, turned, sums)
    outer = matched_halo(prediction[receivers:], weights_ref, offsets_ref, turned)
    for receiver in range(receivers):
        value = recorded_ref[receiver] - added[receiver]
        if receiver == 0:
            value = value - outer[0]
        if receiver == last:
            value = value - outer[1]
        if 0 < receiver < last:
            value = value - inner_ref[receiver - 1]
        out_ref[receiver] = value


def last_kernel(part_ref, ends_ref, out_ref):
    last = out_ref.shape[0] - 1
    out_ref[...] = part_ref[...]
    out_ref[0] = part_ref[0] - ends_ref[0]
    out_ref[last] = part_ref[last] - ends_ref[1]


def call(kernel, arrays, outs, scratch, in_place=0):
    shapes = [s if hasattr(s, "dtype") else jax.ShapeDtypeStruct(s, jnp.float32) for s in outs]
    vmem = pl.BlockSpec(memory_space=pltpu.VMEM)
    return pl.pallas_call(
        kernel,
        out_shape=shapes,
        in_specs=[pl.BlockSpec(memory_space=pl.ANY)] * in_place + [vmem] * (len(arrays) - in_place),
        out_specs=[vmem] * len(shapes),
        scratch_shapes=[
            s if not isinstance(s, tuple) else pltpu.VMEM(s, jnp.float32) for s in scratch
        ],
        compiler_params=pltpu.CompilerParams(vmem_limit_bytes=VMEM_LIMIT),
    )(*arrays)


def local(rows, columns, rb_data, bs_data, recorded, filters, offsets):
    receivers, left_count, samples = rb_data.shape
    right_count, sources, _ = bs_data.shape
    near_count, taps = filters.shape[:2]
    slots, blocks = columns // 2, rows // 2
    def permute(array, target):
        pairs = []
        for i in range(rows):
            for j in range(columns):
                to = target(i, j)
                if to is not None:
                    pairs.append((i * columns + j, to[0] * columns + to[1]))
        return lax.ppermute(array, AXES, pairs)

    def is_same(i, j):
        return i // blocks == j // slots

    cut = 2 * blocks // 3 + 1
    width = 2 * samples
    held = slots * left_count
    one = permute(
        rb_data, lambda i, j: (i, j ^ slots) if is_same(i, j) else (i ^ blocks, j)
    )
    some = [permute(bs_data, lambda i, j, k=k: (i ^ k, j)) for k in range(cut - 1, 0, -1)]
    heres = [rb_data] + [
        permute(rb_data, lambda i, j, k=k: (i, j ^ k)) for k in range(1, slots)
    ]
    table = jax.ShapeDtypeStruct((samples, width), jnp.bfloat16)
    left_shape = (receivers, left_count, width + samples)
    high, low, weights, here_spectra, right_a = call(
        first_kernel,
        [jnp.asarray(phases(samples)), filters.transpose(0, 2, 3, 1), rb_data, bs_data],
        [
            table, table, (tap_rows(near_count, taps)[1], LANES), left_shape,
            (right_count, sources, width),
        ],
        [(LANES, LANES)],
    )
    one, some, heres, high, low, weights, here_spectra, right_a = lax.optimization_barrier(
        (one, some, heres, high, low, weights, here_spectra, right_a)
    )
    some = some[::-1]
    two = permute(one, lambda i, j: (i, j ^ slots) if is_same(i, j) else None)
    ones = [permute(one, lambda i, j, k=k: (i, j ^ k)) for k in range(1, slots)]
    rest = []
    for k in range(cut, blocks):
        bits = [1 << n for n in range(blocks) if 0 < k ^ (1 << n) < cut][:2]
        part = right_count // len(bits)
        for n, bit in enumerate(bits):
            of = some[(k ^ bit) - 1][n * part : (n + 1) * part if n + 1 < len(bits) else None]
            rest.append(permute(of, lambda i, j, bit=bit: (i ^ bit, j)))
    mirror_weights = permute(weights, lambda i, j: (i ^ blocks, j))
    one_spectra, right_b = call(
        second_kernel, [high, low, one] + some,
        [left_shape, (len(some) * right_count, sources, width)], [],
    )
    two, ones, mirror_weights, one_spectra, right_b = lax.optimization_barrier(
        (two, ones, mirror_weights, one_spectra, right_b)
    )
    gathered = [two]
    for k in range(1, slots):
        gathered += [heres[k], ones[k - 1]]
        gathered.append(permute(two, lambda i, j, k=k: None if is_same(i, j) else (i, j ^ k)))
    gathered, rest = lax.optimization_barrier((gathered, rest))
    edge_shape = (2, held, samples)
    near, far = call(
        functools.partial(edge_kernel, slots, blocks), [rb_data, one] + gathered,
        [edge_shape, edge_shape], [],
    )

    def in_half(i, at):
        return at % blocks + i // blocks * blocks

    near = permute(near, lambda i, j: (i ^ 1, j))
    far = permute(far, lambda i, j: (in_half(i, i + 1 if i % 2 else i - 1), j))
    per = samples * receivers * sources // LANES
    right_shape = (blocks * right_count, sources, width + samples)
    own_shape = (receivers, held, width + samples)

    def scratch_of(predicted):
        return [(predicted, sources, width), (predicted, sources, samples), (per + 2 * LANES, LANES)]

    sums = [(near_count, per, LANES)]
    taken = [pltpu.SMEM(offsets.shape, jnp.int32), pltpu.SemaphoreType.DMA(())]
    ones_twos = [two]
    heres_ones = []
    for k in range(1, slots):
        ones_twos += gathered[3 * k - 1 : 3 * k + 1]
        heres_ones += gathered[3 * k - 2 : 3 * k]
    ends_shape = (2, sources, samples)
    ends, inner, right = call(
        functools.partial(main_kernel, slots, blocks),
        [offsets, high, low, mirror_weights, right_a, right_b, one_spectra] + ones_twos + rest,
        [ends_shape, (receivers - 2, sources, samples), right_shape],
        scratch_of(receivers) + sums + taken + [own_shape],
        in_place=1,
    )
    inner = permute(inner, lambda i, j: (i ^ blocks, j))
    ends, halo = call(
        functools.partial(mirror_kernel, blocks),
        [offsets, high, low, mirror_weights, near, far, ends, right],
        [ends_shape, (4, held, width + samples)],
        scratch_of(2) + taken + [(4, held, samples)],
        in_place=1,
    )
    ends = permute(ends, lambda i, j: (i ^ blocks, j))
    (own_part,) = call(
        functools.partial(own_kernel, slots, blocks),
        [offsets, high, low, weights, right, halo, recorded, inner, here_spectra, one_spectra]
        + heres_ones,
        [recorded.shape],
        scratch_of(receivers + 2) + sums + taken + [own_shape],
        in_place=1,
    )
    (out,) = call(last_kernel, [own_part, ends], [recorded.shape], [])
    return out


def solution(mesh):
    in_specs = (
        P("rcv", "src", None),
        P("rcv", "src", None),
        P("rcv", "src", None),
        P(None, None, "rcv", "src"),
        P(),
    )
    out_specs = P("rcv", "src", None)
    body = functools.partial(local, mesh.shape["rcv"], mesh.shape["src"])
    return jax.shard_map(body, mesh=mesh, in_specs=in_specs, out_specs=out_specs, check_vma=False)
```

```python
import functools
import math

import jax
import jax.numpy as jnp
import numpy as np
from jax import lax
from jax.experimental import pallas as pl
from jax.experimental.pallas import tpu as pltpu
from jax.sharding import PartitionSpec as P

LANES = 128
SUBLANES = 8
VMEM_LIMIT = 20 * 1024 * 1024
AXES = ("rcv", "src")
STEP = 32
GROUP = 6
CHUNK = 64


def phases(samples):
    fine = np.arange(STEP, dtype=np.int64)
    coarse = np.arange(0, samples, STEP, dtype=np.int64)
    times = np.concatenate([coarse, fine])[:, None]
    odd = 2 * np.arange(samples, dtype=np.int64)[None, :] + 1
    phase = (times * odd % (4 * samples)).astype(np.float64) * (math.pi / (2 * samples))
    return np.concatenate([np.cos(phase), np.sin(phase)], axis=0).astype(np.float32)


def dft_tables(high_ref, low_ref, phases_ref):
    samples = high_ref.shape[0]
    coarse = samples // STEP
    half = phases_ref.shape[0] // 2
    cos_fine = phases_ref[coarse:half]
    sin_fine = phases_ref[half + coarse :]
    for step in range(coarse):
        cos_step = phases_ref[step : step + 1]
        sin_step = phases_ref[half + step : half + step + 1]
        cosine = cos_step * cos_fine - sin_step * sin_fine
        sine = sin_step * cos_fine + cos_step * sin_fine
        for value, at in ((cosine, 0), (-sine, samples)):
            high = value.astype(jnp.bfloat16)
            where = (pl.ds(step * STEP, STEP), pl.ds(at, samples))
            high_ref[where] = high
            low_ref[where] = (value - high.astype(jnp.float32)).astype(jnp.bfloat16)


def split_dot(rows, high_table, low_table, of=0):
    high = rows.astype(jnp.bfloat16)
    low = (rows - high.astype(jnp.float32)).astype(jnp.bfloat16)

    def dot(left, right):
        return lax.dot_general(
            left, right, (((1,), (of,)), ((), ())), preferred_element_type=jnp.float32
        )

    return dot(high, high_table) + (dot(low, high_table) + dot(high, low_table))


def spectra(traces_ref, tables):
    lead = traces_ref.shape[:-1]
    samples = traces_ref.shape[-1]
    rows = math.prod(lead)
    return split_dot(traces_ref[...].reshape(rows, samples), *tables).reshape(lead + (2 * samples,))


def all_spectra(values, tables):
    rows = [math.prod(value.shape[:-1]) for value in values]
    samples = values[0].shape[-1]
    flat = split_dot(
        jnp.concatenate([value.reshape(-1, samples) for value in values]), *tables
    )
    starts = [sum(rows[:index]) for index in range(len(rows))]
    return [
        flat[start : start + count].reshape(value.shape[:-1] + (2 * samples,))
        for start, count, value in zip(starts, rows, values)
    ]


def with_sums(values):
    half = values.shape[-1] // 2
    total = values[..., :half] + values[..., half:]
    return jnp.concatenate([values, total], axis=-1)


def with_differences(values):
    half = values.shape[-1] // 2
    real, imag = values[..., :half], values[..., half:]
    return jnp.concatenate([real, imag - real, imag + real], axis=-1)


def products(total_ref, lefts, right_ref):
    _, sources, width = total_ref.shape
    half = width // 2
    zero = jnp.zeros((sources, LANES), jnp.float32)
    for tile in range(half // LANES):
        real = pl.ds(tile * LANES, LANES)
        imag = pl.ds(half + tile * LANES, LANES)
        both = pl.ds(width + tile * LANES, LANES)
        for group in range(0, len(lefts), GROUP):
            members = lefts[group : group + GROUP]
            sums = [(zero, zero, zero) for _ in members]
            for bounce in range(right_ref.shape[0]):
                at = slice(bounce, bounce + 1)
                right_real = right_ref[bounce, :, real]
                right_more = right_ref[bounce, :, imag]
                right_both = right_ref[bounce, :, both]
                for index, (_, left_ref, row) in enumerate(members):
                    one, two, three = sums[index]
                    sums[index] = (
                        one + left_ref[row, at, both] * right_real,
                        two + left_ref[row, at, real] * right_more,
                        three + left_ref[row, at, imag] * right_both,
                    )
            for (one, two, three), (row, _, _) in zip(sums, members):
                total_ref[row, :, real] = one - three
                total_ref[row, :, imag] = one + two


def to_traces(prediction_ref, total_ref, tables):
    rows, sources, width = total_ref.shape
    flat = total_ref[...].reshape(rows * sources, width) * (2.0 / width)
    prediction_ref[...] = split_dot(flat, *tables, of=1).reshape(prediction_ref.shape)


def tap_rows(near, taps):
    inner = -(-near * taps // SUBLANES) * SUBLANES
    return inner, inner + -(-taps // SUBLANES) * SUBLANES


def lay_weights(weights_ref, scratch, filters_ref):
    near, receivers, sources, taps = filters_ref.shape
    inner, rows = tap_rows(near, taps)
    scratch[...] = jnp.zeros(scratch.shape, jnp.float32)
    lanes = receivers * sources
    for copy in range(LANES // lanes):
        for step in range(near):
            for row in range(receivers):
                receiver = row + 1 - step
                if 0 <= receiver < receivers:
                    at = pl.ds(copy * lanes + row * sources, sources)
                    scratch[at, step * taps : (step + 1) * taps] = filters_ref[step, receiver]
    for copy in range(LANES // (2 * sources)):
        for row, value in enumerate((filters_ref[0, 0], filters_ref[near - 1, receivers - 1])):
            at = pl.ds((copy * 2 + row) * sources, sources)
            scratch[at, inner : inner + taps] = value
    weights_ref[...] = scratch[...].T[:rows]


def turn(turned, prediction):
    receivers, sources, samples = prediction.shape
    lanes = receivers * sources
    per = samples * lanes // LANES
    zero = jnp.zeros((lanes, LANES), jnp.float32)
    for block in range(per // LANES + 2):
        side = []
        for start in range(0, samples, per):
            at = start + (block - 1) * LANES
            if 0 <= at < samples:
                side.append(prediction[:, :, at : at + LANES].reshape(lanes, LANES))
            else:
                side.append(zero)
        turned[pl.ds(block * LANES, LANES)] = jnp.concatenate(side, axis=0).T


def turn_back(value, receivers, sources):
    per = value.shape[0]
    parts = LANES // (receivers * sources)
    back = jnp.concatenate([value[at : at + LANES].T for at in range(0, per, LANES)], axis=1)
    back = back.reshape(parts, receivers, sources, per)
    return jnp.concatenate([back[part] for part in range(parts)], axis=2)


def matched(prediction, weights_ref, offsets_ref, turned, sums):
    receivers, sources, samples = prediction.shape
    near, taps = sums.shape[0], offsets_ref.shape[0]
    per = samples * receivers * sources // LANES
    turn(turned, prediction)
    chunk = min(per, CHUNK)
    for first in range(0, per, chunk):
        totals = [jnp.zeros((chunk, LANES), jnp.float32) for _ in range(near)]
        for tap in range(taps):
            shifted = turned[pl.ds(LANES + first - offsets_ref[tap], chunk), :]
            for step in range(near):
                at = step * taps + tap
                totals[step] = totals[step] + weights_ref[at : at + 1] * shifted
        for step in range(near):
            sums[step, pl.ds(first, chunk)] = totals[step]
    added = [None] * receivers
    for step in range(near):
        back = turn_back(sums[step, pl.ds(0, per)], receivers, sources)
        for row in range(receivers):
            receiver = row + 1 - step
            if 0 <= receiver < receivers:
                before = added[receiver]
                added[receiver] = back[row] if before is None else before + back[row]
    return added


def matched_halo(prediction, weights_ref, offsets_ref, turned):
    two, sources, samples = prediction.shape
    taps = offsets_ref.shape[0]
    first_tap = weights_ref.shape[0] - -(-taps // SUBLANES) * SUBLANES
    per = samples * two * sources // LANES
    turn(turned, prediction)
    total = jnp.zeros((per, LANES), jnp.float32)
    for tap in range(taps):
        shifted = turned[pl.ds(LANES - offsets_ref[tap], per), :]
        total = total + weights_ref[first_tap + tap : first_tap + tap + 1] * shifted
    return turn_back(total, two, sources)


def first_kernel(
    phases_ref, filters_ref, here_ref, right_ref,
    high_ref, low_ref, weights_ref, here_out, right_out, turned,
):
    dft_tables(high_ref, low_ref, phases_ref)
    lay_weights(weights_ref, turned, filters_ref)
    here, right = all_spectra(
        [here_ref[...], right_ref[...]], (high_ref[...], low_ref[...])
    )
    here_out[...] = with_sums(here)
    right_out[...] = right


def second_kernel(high_ref, low_ref, one_ref, *refs):
    right_refs, (one_out, right_out) = refs[:-2], refs[-2:]
    one, *right = all_spectra(
        [one_ref[...]] + [ref[...] for ref in right_refs], (high_ref[...], low_ref[...])
    )
    one_out[...] = with_sums(one)
    held = right_refs[0].shape[0]
    for block, value in enumerate(right):
        right_out[pl.ds(block * held, held)] = value


def position(slots, blocks):
    row, column = lax.axis_index("rcv"), lax.axis_index("src")
    return row, column, row // blocks == column // slots


def place_of(column, slot, slots, held):
    first = jnp.bitwise_xor(column, slot) % slots * held
    return pl.ds(pl.multiple_of(first, held), held)


def edge_kernel(slots, blocks, *refs):
    near_ref, far_ref = refs[3 * slots :]
    row, column, same = position(slots, blocks)
    odd = row % 2 == 1
    receivers, held, _ = refs[0].shape
    for slot in range(slots):
        these = place_of(column, slot, slots, held)
        here, one, two = refs[3 * slot : 3 * slot + 3]
        for index, (yes, no) in enumerate(((here, one), (one, two))):
            first = jnp.where(same, yes[0], no[0])
            last = jnp.where(same, yes[receivers - 1], no[receivers - 1])
            near_ref[index, these] = jnp.where(odd, first, last)
            far_ref[index, these] = jnp.where(odd, last, first)


def main_kernel(
    slots, blocks, offsets_from, high_ref, low_ref, weights_ref, right_a, right_b, one_ref, *refs
):
    columns, refs = refs[: 2 * slots - 1], refs[2 * slots - 1 :]
    right_refs, refs = refs[:-10], refs[-10:]
    ends_ref, out_ref, right_ref, total, prediction, turned, sums, offsets_ref, arrived = refs[:9]
    left_ref = refs[9]
    copy = pltpu.make_async_copy(offsets_from, offsets_ref, arrived)
    copy.start()
    row, column, same = position(slots, blocks)
    count = right_a.shape[0]
    traces = [columns[0][...]]
    for slot in range(1, slots):
        one, two = columns[2 * slot - 1 : 2 * slot + 1]
        traces.append(jnp.where(same, one[...], two[...]))
    spectra_of = all_spectra(
        traces + [ref[...] for ref in right_refs], (high_ref[...], low_ref[...])
    )
    place = 0
    for value in [right_a, right_b] + spectra_of[slots:]:
        step = min(count, value.shape[0])
        for first in range(0, value.shape[0], step):
            at = jnp.bitwise_xor(row, place // count) % blocks * count + place % count
            right_ref[pl.ds(at, step)] = with_differences(value[first : first + step])
            place += step
    receivers, held, _ = one_ref.shape
    for slot in range(slots):
        these = place_of(column, slot, slots, held)
        mirror = with_sums(spectra_of[slot])
        if slot == 0:
            mirror = jnp.where(same, one_ref[...], mirror)
        for receiver in range(receivers):
            left_ref[receiver, these] = mirror[receiver]
    products(total, [(row, left_ref, row) for row in range(receivers)], right_ref)
    to_traces(prediction, total, (high_ref[...], low_ref[...]))
    copy.wait()
    added = matched(prediction, weights_ref, offsets_ref, turned, sums)
    ends_ref[0] = added[0]
    ends_ref[1] = added[-1]
    for receiver in range(1, receivers - 1):
        out_ref[receiver - 1] = added[receiver]


def mirror_kernel(
    blocks, offsets_from, high_ref, low_ref, weights_ref, near_ref, far_ref, part_ref,
    right_ref, out_ref, halo_ref, total, prediction, turned, offsets_ref, arrived, outer,
):
    copy = pltpu.make_async_copy(offsets_from, offsets_ref, arrived)
    copy.start()
    row = lax.axis_index("rcv")
    odd, lower = row % 2 == 1, row < blocks
    before = jnp.where(odd, near_ref[...], far_ref[...])
    after = jnp.where(odd, far_ref[...], near_ref[...])
    zero = jnp.zeros(before.shape[1:], jnp.float32)
    for which, (value, end, none) in enumerate(
        (
            (before, row % blocks == 0, lower),
            (after, row % blocks == blocks - 1, jnp.logical_not(lower)),
        )
    ):
        own, mirror = value[0], value[1]
        outer[which] = jnp.where(end, jnp.where(none, zero, mirror), own)
        outer[2 + which] = jnp.where(end, jnp.where(none, own, zero), mirror)
    tables = (high_ref[...], low_ref[...])
    halo_ref[...] = with_sums(spectra(outer, tables))
    products(total, [(0, halo_ref, 2), (1, halo_ref, 3)], right_ref)
    to_traces(prediction, total, tables)
    copy.wait()
    added = matched_halo(prediction[...], weights_ref, offsets_ref, turned)
    out_ref[...] = part_ref[...] + added


def own_kernel(
    slots, blocks, offsets_from, high_ref, low_ref, weights_ref, right_ref, halo_ref,
    recorded_ref, inner_ref, here_ref, one_ref, *refs
):
    columns, refs = refs[: 2 * slots - 2], refs[2 * slots - 2 :]
    out_ref, total, prediction, turned, sums, offsets_ref, arrived, left_ref = refs
    copy = pltpu.make_async_copy(offsets_from, offsets_ref, arrived)
    copy.start()
    tables = (high_ref[...], low_ref[...])
    row, column, same = position(slots, blocks)
    receivers, held, _ = here_ref.shape
    for slot in range(slots):
        these = place_of(column, slot, slots, held)
        if slot == 0:
            own = jnp.where(same, here_ref[...], one_ref[...])
        else:
            here, one = columns[2 * slot - 2 : 2 * slot]
            chosen = jnp.where(same, here[...], one[...])
            own = with_sums(all_spectra([chosen], tables)[0])
        for receiver in range(receivers):
            left_ref[receiver, these] = own[receiver]
    lefts = [(row, left_ref, row) for row in range(receivers)]
    lefts += [(receivers, halo_ref, 0), (receivers + 1, halo_ref, 1)]
    products(total, lefts, right_ref)
    to_traces(prediction, total, tables)
    copy.wait()
    last = receivers - 1
    added = matched(prediction[:receivers], weights_ref, offsets_ref, turned, sums)
    outer = matched_halo(prediction[receivers:], weights_ref, offsets_ref, turned)
    for receiver in range(receivers):
        value = recorded_ref[receiver] - added[receiver]
        if receiver == 0:
            value = value - outer[0]
        if receiver == last:
            value = value - outer[1]
        if 0 < receiver < last:
            value = value - inner_ref[receiver - 1]
        out_ref[receiver] = value


def last_kernel(part_ref, ends_ref, out_ref):
    last = out_ref.shape[0] - 1
    out_ref[...] = part_ref[...]
    out_ref[0] = part_ref[0] - ends_ref[0]
    out_ref[last] = part_ref[last] - ends_ref[1]


def call(kernel, arrays, outs, scratch, in_place=0):
    shapes = [s if hasattr(s, "dtype") else jax.ShapeDtypeStruct(s, jnp.float32) for s in outs]
    vmem = pl.BlockSpec(memory_space=pltpu.VMEM)
    return pl.pallas_call(
        kernel,
        out_shape=shapes,
        in_specs=[pl.BlockSpec(memory_space=pl.ANY)] * in_place + [vmem] * (len(arrays) - in_place),
        out_specs=[vmem] * len(shapes),
        scratch_shapes=[
            s if not isinstance(s, tuple) else pltpu.VMEM(s, jnp.float32) for s in scratch
        ],
        compiler_params=pltpu.CompilerParams(vmem_limit_bytes=VMEM_LIMIT),
    )(*arrays)


def local(rows, columns, rb_data, bs_data, recorded, filters, offsets):
    receivers, left_count, samples = rb_data.shape
    right_count, sources, _ = bs_data.shape
    near_count, taps = filters.shape[:2]
    slots, blocks = columns // 2, rows // 2
    def permute(array, target):
        pairs = []
        for i in range(rows):
            for j in range(columns):
                to = target(i, j)
                if to is not None:
                    pairs.append((i * columns + j, to[0] * columns + to[1]))
        return lax.ppermute(array, AXES, pairs)

    def is_same(i, j):
        return i // blocks == j // slots

    cut = 2 * blocks // 3 + 1
    width = 2 * samples
    held = slots * left_count
    one = permute(
        rb_data, lambda i, j: (i, j ^ slots) if is_same(i, j) else (i ^ blocks, j)
    )
    some = [permute(bs_data, lambda i, j, k=k: (i ^ k, j)) for k in range(cut - 1, 0, -1)]
    heres = [rb_data] + [
        permute(rb_data, lambda i, j, k=k: (i, j ^ k)) for k in range(1, slots)
    ]
    table = jax.ShapeDtypeStruct((samples, width), jnp.bfloat16)
    left_shape = (receivers, left_count, width + samples)
    high, low, weights, here_spectra, right_a = call(
        first_kernel,
        [jnp.asarray(phases(samples)), filters.transpose(0, 2, 3, 1), rb_data, bs_data],
        [
            table, table, (tap_rows(near_count, taps)[1], LANES), left_shape,
            (right_count, sources, width),
        ],
        [(LANES, LANES)],
    )
    one, some, heres, high, low, weights, here_spectra, right_a = lax.optimization_barrier(
        (one, some, heres, high, low, weights, here_spectra, right_a)
    )
    some = some[::-1]
    two = permute(one, lambda i, j: (i, j ^ slots) if is_same(i, j) else None)
    ones = [permute(one, lambda i, j, k=k: (i, j ^ k)) for k in range(1, slots)]
    rest = []
    for k in range(cut, blocks):
        bits = [1 << n for n in range(blocks) if 0 < k ^ (1 << n) < cut][1::-1]
        part = right_count // len(bits)
        for n, bit in enumerate(bits):
            of = some[(k ^ bit) - 1][n * part : (n + 1) * part if n + 1 < len(bits) else None]
            rest.append(permute(of, lambda i, j, bit=bit: (i ^ bit, j)))
    mirror_weights = permute(weights, lambda i, j: (i ^ blocks, j))
    one_spectra, right_b = call(
        second_kernel, [high, low, one] + some,
        [left_shape, (len(some) * right_count, sources, width)], [],
    )
    ones, two, mirror_weights, one_spectra, right_b = lax.optimization_barrier(
        (ones, two, mirror_weights, one_spectra, right_b)
    )
    gathered = [two]
    for k in range(1, slots):
        gathered += [heres[k], ones[k - 1]]
        gathered.append(permute(two, lambda i, j, k=k: None if is_same(i, j) else (i, j ^ k)))
    gathered, rest = lax.optimization_barrier((gathered, rest))
    edge_shape = (2, held, samples)
    near, far = call(
        functools.partial(edge_kernel, slots, blocks), [rb_data, one] + gathered,
        [edge_shape, edge_shape], [],
    )

    def in_half(i, at):
        return at % blocks + i // blocks * blocks

    near = permute(near, lambda i, j: (i ^ 1, j))
    far = permute(far, lambda i, j: (in_half(i, i + 1 if i % 2 else i - 1), j))
    per = samples * receivers * sources // LANES
    right_shape = (blocks * right_count, sources, width + samples)
    own_shape = (receivers, held, width + samples)

    def scratch_of(predicted):
        return [(predicted, sources, width), (predicted, sources, samples), (per + 2 * LANES, LANES)]

    sums = [(near_count, per, LANES)]
    taken = [pltpu.SMEM(offsets.shape, jnp.int32), pltpu.SemaphoreType.DMA(())]
    ones_twos = [two]
    heres_ones = []
    for k in range(1, slots):
        ones_twos += gathered[3 * k - 1 : 3 * k + 1]
        heres_ones += gathered[3 * k - 2 : 3 * k]
    ends_shape = (2, sources, samples)
    ends, inner, right = call(
        functools.partial(main_kernel, slots, blocks),
        [offsets, high, low, mirror_weights, right_a, right_b, one_spectra] + ones_twos + rest,
        [ends_shape, (receivers - 2, sources, samples), right_shape],
        scratch_of(receivers) + sums + taken + [own_shape],
        in_place=1,
    )
    inner = permute(inner, lambda i, j: (i ^ blocks, j))
    ends, halo = call(
        functools.partial(mirror_kernel, blocks),
        [offsets, high, low, mirror_weights, near, far, ends, right],
        [ends_shape, (4, held, width + samples)],
        scratch_of(2) + taken + [(4, held, samples)],
        in_place=1,
    )
    ends = permute(ends, lambda i, j: (i ^ blocks, j))
    (own_part,) = call(
        functools.partial(own_kernel, slots, blocks),
        [offsets, high, low, weights, right, halo, recorded, inner, here_spectra, one_spectra]
        + heres_ones,
        [recorded.shape],
        scratch_of(receivers + 2) + sums + taken + [own_shape],
        in_place=1,
    )
    (out,) = call(last_kernel, [own_part, ends], [recorded.shape], [])
    return out


def solution(mesh):
    in_specs = (
        P("rcv", "src", None),
        P("rcv", "src", None),
        P("rcv", "src", None),
        P(None, None, "rcv", "src"),
        P(),
    )
    out_specs = P("rcv", "src", None)
    body = functools.partial(local, mesh.shape["rcv"], mesh.shape["src"])
    return jax.shard_map(body, mesh=mesh, in_specs=in_specs, out_specs=out_specs, check_vma=False)
```

```python
import functools
import math

import jax
import jax.numpy as jnp
import numpy as np
from jax import lax
from jax.experimental import pallas as pl
from jax.experimental.pallas import tpu as pltpu
from jax.sharding import PartitionSpec as P

LANES = 128
SUBLANES = 8
VMEM_LIMIT = 20 * 1024 * 1024
AXES = ("rcv", "src")
STEP = 32
GROUP = 6
CHUNK = 128


def phases(samples):
    fine = np.arange(STEP, dtype=np.int64)
    coarse = np.arange(0, samples, STEP, dtype=np.int64)
    times = np.concatenate([coarse, fine])[:, None]
    odd = 2 * np.arange(samples, dtype=np.int64)[None, :] + 1
    phase = (times * odd % (4 * samples)).astype(np.float64) * (math.pi / (2 * samples))
    return np.concatenate([np.cos(phase), np.sin(phase)], axis=0).astype(np.float32)


def dft_tables(high_ref, low_ref, phases_ref):
    samples = high_ref.shape[0]
    coarse = samples // STEP
    half = phases_ref.shape[0] // 2
    cos_fine = phases_ref[coarse:half]
    sin_fine = phases_ref[half + coarse :]
    for step in range(coarse):
        cos_step = phases_ref[step : step + 1]
        sin_step = phases_ref[half + step : half + step + 1]
        cosine = cos_step * cos_fine - sin_step * sin_fine
        sine = sin_step * cos_fine + cos_step * sin_fine
        for value, at in ((cosine, 0), (-sine, samples)):
            high = value.astype(jnp.bfloat16)
            where = (pl.ds(step * STEP, STEP), pl.ds(at, samples))
            high_ref[where] = high
            low_ref[where] = (value - high.astype(jnp.float32)).astype(jnp.bfloat16)


def split_dot(rows, high_table, low_table, of=0):
    high = rows.astype(jnp.bfloat16)
    low = (rows - high.astype(jnp.float32)).astype(jnp.bfloat16)

    def dot(left, right):
        return lax.dot_general(
            left, right, (((1,), (of,)), ((), ())), preferred_element_type=jnp.float32
        )

    return dot(high, high_table) + (dot(low, high_table) + dot(high, low_table))


def spectra(traces_ref, tables):
    lead = traces_ref.shape[:-1]
    samples = traces_ref.shape[-1]
    rows = math.prod(lead)
    return split_dot(traces_ref[...].reshape(rows, samples), *tables).reshape(lead + (2 * samples,))


def all_spectra(values, tables):
    rows = [math.prod(value.shape[:-1]) for value in values]
    samples = values[0].shape[-1]
    flat = split_dot(
        jnp.concatenate([value.reshape(-1, samples) for value in values]), *tables
    )
    starts = [sum(rows[:index]) for index in range(len(rows))]
    return [
        flat[start : start + count].reshape(value.shape[:-1] + (2 * samples,))
        for start, count, value in zip(starts, rows, values)
    ]


def with_sums(values):
    half = values.shape[-1] // 2
    total = values[..., :half] + values[..., half:]
    return jnp.concatenate([values, total], axis=-1)


def with_differences(values):
    half = values.shape[-1] // 2
    real, imag = values[..., :half], values[..., half:]
    return jnp.concatenate([real, imag - real, imag + real], axis=-1)


def products(total_ref, lefts, right_ref):
    _, sources, width = total_ref.shape
    half = width // 2
    zero = jnp.zeros((sources, LANES), jnp.float32)
    for tile in range(half // LANES):
        real = pl.ds(tile * LANES, LANES)
        imag = pl.ds(half + tile * LANES, LANES)
        both = pl.ds(width + tile * LANES, LANES)
        for group in range(0, len(lefts), GROUP):
            members = lefts[group : group + GROUP]
            sums = [(zero, zero, zero) for _ in members]
            for bounce in range(right_ref.shape[0]):
                at = slice(bounce, bounce + 1)
                right_real = right_ref[bounce, :, real]
                right_more = right_ref[bounce, :, imag]
                right_both = right_ref[bounce, :, both]
                for index, (_, left_ref, row) in enumerate(members):
                    one, two, three = sums[index]
                    sums[index] = (
                        one + left_ref[row, at, both] * right_real,
                        two + left_ref[row, at, real] * right_more,
                        three + left_ref[row, at, imag] * right_both,
                    )
            for (one, two, three), (row, _, _) in zip(sums, members):
                total_ref[row, :, real] = one - three
                total_ref[row, :, imag] = one + two


def to_traces(prediction_ref, total_ref, tables):
    rows, sources, width = total_ref.shape
    flat = total_ref[...].reshape(rows * sources, width) * (2.0 / width)
    prediction_ref[...] = split_dot(flat, *tables, of=1).reshape(prediction_ref.shape)


def tap_rows(near, taps):
    inner = -(-near * taps // SUBLANES) * SUBLANES
    return inner, inner + -(-taps // SUBLANES) * SUBLANES


def lay_weights(weights_ref, scratch, filters_ref):
    near, receivers, sources, taps = filters_ref.shape
    inner, rows = tap_rows(near, taps)
    scratch[...] = jnp.zeros(scratch.shape, jnp.float32)
    lanes = receivers * sources
    for copy in range(LANES // lanes):
        for step in range(near):
            for row in range(receivers):
                receiver = row + 1 - step
                if 0 <= receiver < receivers:
                    at = pl.ds(copy * lanes + row * sources, sources)
                    scratch[at, step * taps : (step + 1) * taps] = filters_ref[step, receiver]
    for copy in range(LANES // (2 * sources)):
        for row, value in enumerate((filters_ref[0, 0], filters_ref[near - 1, receivers - 1])):
            at = pl.ds((copy * 2 + row) * sources, sources)
            scratch[at, inner : inner + taps] = value
    weights_ref[...] = scratch[...].T[:rows]


def turn(turned, prediction):
    receivers, sources, samples = prediction.shape
    lanes = receivers * sources
    per = samples * lanes // LANES
    zero = jnp.zeros((lanes, LANES), jnp.float32)
    for block in range(per // LANES + 2):
        side = []
        for start in range(0, samples, per):
            at = start + (block - 1) * LANES
            if 0 <= at < samples:
                side.append(prediction[:, :, at : at + LANES].reshape(lanes, LANES))
            else:
                side.append(zero)
        turned[pl.ds(block * LANES, LANES)] = jnp.concatenate(side, axis=0).T


def turn_back(value, receivers, sources):
    per = value.shape[0]
    parts = LANES // (receivers * sources)
    back = jnp.concatenate([value[at : at + LANES].T for at in range(0, per, LANES)], axis=1)
    back = back.reshape(parts, receivers, sources, per)
    return jnp.concatenate([back[part] for part in range(parts)], axis=2)


def matched(prediction, weights_ref, offsets_ref, turned, sums):
    receivers, sources, samples = prediction.shape
    near, taps = sums.shape[0], offsets_ref.shape[0]
    per = samples * receivers * sources // LANES
    turn(turned, prediction)
    chunk = min(per, CHUNK)
    for first in range(0, per, chunk):
        totals = [jnp.zeros((chunk, LANES), jnp.float32) for _ in range(near)]
        for tap in range(taps):
            shifted = turned[pl.ds(LANES + first - offsets_ref[tap], chunk), :]
            for step in range(near):
                at = step * taps + tap
                totals[step] = totals[step] + weights_ref[at : at + 1] * shifted
        for step in range(near):
            sums[step, pl.ds(first, chunk)] = totals[step]
    added = [None] * receivers
    for step in range(near):
        back = turn_back(sums[step, pl.ds(0, per)], receivers, sources)
        for row in range(receivers):
            receiver = row + 1 - step
            if 0 <= receiver < receivers:
                before = added[receiver]
                added[receiver] = back[row] if before is None else before + back[row]
    return added


def matched_halo(prediction, weights_ref, offsets_ref, turned):
    two, sources, samples = prediction.shape
    taps = offsets_ref.shape[0]
    first_tap = weights_ref.shape[0] - -(-taps // SUBLANES) * SUBLANES
    per = samples * two * sources // LANES
    turn(turned, prediction)
    total = jnp.zeros((per, LANES), jnp.float32)
    for tap in range(taps):
        shifted = turned[pl.ds(LANES - offsets_ref[tap], per), :]
        total = total + weights_ref[first_tap + tap : first_tap + tap + 1] * shifted
    return turn_back(total, two, sources)


def first_kernel(
    phases_ref, filters_ref, here_ref, right_ref,
    high_ref, low_ref, weights_ref, here_out, right_out, turned,
):
    dft_tables(high_ref, low_ref, phases_ref)
    lay_weights(weights_ref, turned, filters_ref)
    here, right = all_spectra(
        [here_ref[...], right_ref[...]], (high_ref[...], low_ref[...])
    )
    here_out[...] = with_sums(here)
    right_out[...] = right


def second_kernel(high_ref, low_ref, one_ref, *refs):
    right_refs, (one_out, right_out) = refs[:-2], refs[-2:]
    one, *right = all_spectra(
        [one_ref[...]] + [ref[...] for ref in right_refs], (high_ref[...], low_ref[...])
    )
    one_out[...] = with_sums(one)
    held = right_refs[0].shape[0]
    for block, value in enumerate(right):
        right_out[pl.ds(block * held, held)] = value


def position(slots, blocks):
    row, column = lax.axis_index("rcv"), lax.axis_index("src")
    return row, column, row // blocks == column // slots


def place_of(column, slot, slots, held):
    first = jnp.bitwise_xor(column, slot) % slots * held
    return pl.ds(pl.multiple_of(first, held), held)


def edge_kernel(slots, blocks, *refs):
    near_ref, far_ref = refs[3 * slots :]
    row, column, same = position(slots, blocks)
    odd = row % 2 == 1
    receivers, held, _ = refs[0].shape
    for slot in range(slots):
        these = place_of(column, slot, slots, held)
        here, one, two = refs[3 * slot : 3 * slot + 3]
        for index, (yes, no) in enumerate(((here, one), (one, two))):
            first = jnp.where(same, yes[0], no[0])
            last = jnp.where(same, yes[receivers - 1], no[receivers - 1])
            near_ref[index, these] = jnp.where(odd, first, last)
            far_ref[index, these] = jnp.where(odd, last, first)


def main_kernel(
    slots, blocks, offsets_from, high_ref, low_ref, weights_ref, right_a, right_b, one_ref, *refs
):
    columns, refs = refs[: 2 * slots - 1], refs[2 * slots - 1 :]
    right_refs, refs = refs[:-10], refs[-10:]
    ends_ref, out_ref, right_ref, total, prediction, turned, sums, offsets_ref, arrived = refs[:9]
    left_ref = refs[9]
    copy = pltpu.make_async_copy(offsets_from, offsets_ref, arrived)
    copy.start()
    row, column, same = position(slots, blocks)
    count = right_a.shape[0]
    traces = [columns[0][...]]
    for slot in range(1, slots):
        one, two = columns[2 * slot - 1 : 2 * slot + 1]
        traces.append(jnp.where(same, one[...], two[...]))
    spectra_of = all_spectra(
        traces + [ref[...] for ref in right_refs], (high_ref[...], low_ref[...])
    )
    place = 0
    for value in [right_a, right_b] + spectra_of[slots:]:
        step = min(count, value.shape[0])
        for first in range(0, value.shape[0], step):
            at = jnp.bitwise_xor(row, place // count) % blocks * count + place % count
            right_ref[pl.ds(at, step)] = with_differences(value[first : first + step])
            place += step
    receivers, held, _ = one_ref.shape
    for slot in range(slots):
        these = place_of(column, slot, slots, held)
        mirror = with_sums(spectra_of[slot])
        if slot == 0:
            mirror = jnp.where(same, one_ref[...], mirror)
        for receiver in range(receivers):
            left_ref[receiver, these] = mirror[receiver]
    products(total, [(row, left_ref, row) for row in range(receivers)], right_ref)
    to_traces(prediction, total, (high_ref[...], low_ref[...]))
    copy.wait()
    added = matched(prediction, weights_ref, offsets_ref, turned, sums)
    ends_ref[0] = added[0]
    ends_ref[1] = added[-1]
    for receiver in range(1, receivers - 1):
        out_ref[receiver - 1] = added[receiver]


def mirror_kernel(
    blocks, offsets_from, high_ref, low_ref, weights_ref, near_ref, far_ref, part_ref,
    right_ref, out_ref, halo_ref, total, prediction, turned, offsets_ref, arrived, outer,
):
    copy = pltpu.make_async_copy(offsets_from, offsets_ref, arrived)
    copy.start()
    row = lax.axis_index("rcv")
    odd, lower = row % 2 == 1, row < blocks
    before = jnp.where(odd, near_ref[...], far_ref[...])
    after = jnp.where(odd, far_ref[...], near_ref[...])
    zero = jnp.zeros(before.shape[1:], jnp.float32)
    for which, (value, end, none) in enumerate(
        (
            (before, row % blocks == 0, lower),
            (after, row % blocks == blocks - 1, jnp.logical_not(lower)),
        )
    ):
        own, mirror = value[0], value[1]
        outer[which] = jnp.where(end, jnp.where(none, zero, mirror), own)
        outer[2 + which] = jnp.where(end, jnp.where(none, own, zero), mirror)
    tables = (high_ref[...], low_ref[...])
    halo_ref[...] = with_sums(spectra(outer, tables))
    products(total, [(0, halo_ref, 2), (1, halo_ref, 3)], right_ref)
    to_traces(prediction, total, tables)
    copy.wait()
    added = matched_halo(prediction[...], weights_ref, offsets_ref, turned)
    out_ref[...] = part_ref[...] + added


def own_kernel(
    slots, blocks, offsets_from, high_ref, low_ref, weights_ref, right_ref, halo_ref,
    recorded_ref, inner_ref, here_ref, one_ref, *refs
):
    columns, refs = refs[: 2 * slots - 2], refs[2 * slots - 2 :]
    out_ref, total, prediction, turned, sums, offsets_ref, arrived, left_ref = refs
    copy = pltpu.make_async_copy(offsets_from, offsets_ref, arrived)
    copy.start()
    tables = (high_ref[...], low_ref[...])
    row, column, same = position(slots, blocks)
    receivers, held, _ = here_ref.shape
    for slot in range(slots):
        these = place_of(column, slot, slots, held)
        if slot == 0:
            own = jnp.where(same, here_ref[...], one_ref[...])
        else:
            here, one = columns[2 * slot - 2 : 2 * slot]
            chosen = jnp.where(same, here[...], one[...])
            own = with_sums(all_spectra([chosen], tables)[0])
        for receiver in range(receivers):
            left_ref[receiver, these] = own[receiver]
    lefts = [(row, left_ref, row) for row in range(receivers)]
    lefts += [(receivers, halo_ref, 0), (receivers + 1, halo_ref, 1)]
    products(total, lefts, right_ref)
    to_traces(prediction, total, tables)
    copy.wait()
    last = receivers - 1
    added = matched(prediction[:receivers], weights_ref, offsets_ref, turned, sums)
    outer = matched_halo(prediction[receivers:], weights_ref, offsets_ref, turned)
    for receiver in range(receivers):
        value = recorded_ref[receiver] - added[receiver]
        if receiver == 0:
            value = value - outer[0]
        if receiver == last:
            value = value - outer[1]
        if 0 < receiver < last:
            value = value - inner_ref[receiver - 1]
        out_ref[receiver] = value


def last_kernel(part_ref, ends_ref, out_ref):
    last = out_ref.shape[0] - 1
    out_ref[...] = part_ref[...]
    out_ref[0] = part_ref[0] - ends_ref[0]
    out_ref[last] = part_ref[last] - ends_ref[1]


def call(kernel, arrays, outs, scratch, in_place=0):
    shapes = [s if hasattr(s, "dtype") else jax.ShapeDtypeStruct(s, jnp.float32) for s in outs]
    vmem = pl.BlockSpec(memory_space=pltpu.VMEM)
    return pl.pallas_call(
        kernel,
        out_shape=shapes,
        in_specs=[pl.BlockSpec(memory_space=pl.ANY)] * in_place + [vmem] * (len(arrays) - in_place),
        out_specs=[vmem] * len(shapes),
        scratch_shapes=[
            s if not isinstance(s, tuple) else pltpu.VMEM(s, jnp.float32) for s in scratch
        ],
        compiler_params=pltpu.CompilerParams(vmem_limit_bytes=VMEM_LIMIT),
    )(*arrays)


def local(rows, columns, rb_data, bs_data, recorded, filters, offsets):
    receivers, left_count, samples = rb_data.shape
    right_count, sources, _ = bs_data.shape
    near_count, taps = filters.shape[:2]
    slots, blocks = columns // 2, rows // 2
    def permute(array, target):
        pairs = []
        for i in range(rows):
            for j in range(columns):
                to = target(i, j)
                if to is not None:
                    pairs.append((i * columns + j, to[0] * columns + to[1]))
        return lax.ppermute(array, AXES, pairs)

    def is_same(i, j):
        return i // blocks == j // slots

    cut = 2 * blocks // 3 + 1
    width = 2 * samples
    held = slots * left_count
    one = permute(
        rb_data, lambda i, j: (i, j ^ slots) if is_same(i, j) else (i ^ blocks, j)
    )
    some = [permute(bs_data, lambda i, j, k=k: (i ^ k, j)) for k in range(cut - 1, 0, -1)]
    heres = [rb_data] + [
        permute(rb_data, lambda i, j, k=k: (i, j ^ k)) for k in range(1, slots)
    ]
    table = jax.ShapeDtypeStruct((samples, width), jnp.bfloat16)
    left_shape = (receivers, left_count, width + samples)
    high, low, weights, here_spectra, right_a = call(
        first_kernel,
        [jnp.asarray(phases(samples)), filters.transpose(0, 2, 3, 1), rb_data, bs_data],
        [
            table, table, (tap_rows(near_count, taps)[1], LANES), left_shape,
            (right_count, sources, width),
        ],
        [(LANES, LANES)],
    )
    one, some, heres, high, low, weights, here_spectra, right_a = lax.optimization_barrier(
        (one, some, heres, high, low, weights, here_spectra, right_a)
    )
    some = some[::-1]
    two = permute(one, lambda i, j: (i, j ^ slots) if is_same(i, j) else None)
    ones = [permute(one, lambda i, j, k=k: (i, j ^ k)) for k in range(1, slots)]
    rest = []
    for k in range(cut, blocks):
        bits = [1 << n for n in range(blocks) if 0 < k ^ (1 << n) < cut][:2]
        part = right_count // len(bits)
        for n, bit in enumerate(bits):
            of = some[(k ^ bit) - 1][n * part : (n + 1) * part if n + 1 < len(bits) else None]
            rest.append(permute(of, lambda i, j, bit=bit: (i ^ bit, j)))
    mirror_weights = permute(weights, lambda i, j: (i ^ blocks, j))
    one_spectra, right_b = call(
        second_kernel, [high, low, one] + some,
        [left_shape, (len(some) * right_count, sources, width)], [],
    )
    two, ones, mirror_weights, one_spectra, right_b = lax.optimization_barrier(
        (two, ones, mirror_weights, one_spectra, right_b)
    )
    gathered = [two]
    for k in range(1, slots):
        gathered += [heres[k], ones[k - 1]]
        gathered.append(permute(two, lambda i, j, k=k: None if is_same(i, j) else (i, j ^ k)))
    gathered, rest = lax.optimization_barrier((gathered, rest))
    edge_shape = (2, held, samples)
    near, far = call(
        functools.partial(edge_kernel, slots, blocks), [rb_data, one] + gathered,
        [edge_shape, edge_shape], [],
    )

    def in_half(i, at):
        return at % blocks + i // blocks * blocks

    near = permute(near, lambda i, j: (i ^ 1, j))
    far = permute(far, lambda i, j: (in_half(i, i + 1 if i % 2 else i - 1), j))
    per = samples * receivers * sources // LANES
    right_shape = (blocks * right_count, sources, width + samples)
    own_shape = (receivers, held, width + samples)

    def scratch_of(predicted):
        return [(predicted, sources, width), (predicted, sources, samples), (per + 2 * LANES, LANES)]

    sums = [(near_count, per, LANES)]
    taken = [pltpu.SMEM(offsets.shape, jnp.int32), pltpu.SemaphoreType.DMA(())]
    ones_twos = [two]
    heres_ones = []
    for k in range(1, slots):
        ones_twos += gathered[3 * k - 1 : 3 * k + 1]
        heres_ones += gathered[3 * k - 2 : 3 * k]
    ends_shape = (2, sources, samples)
    ends, inner, right = call(
        functools.partial(main_kernel, slots, blocks),
        [offsets, high, low, mirror_weights, right_a, right_b, one_spectra] + ones_twos + rest,
        [ends_shape, (receivers - 2, sources, samples), right_shape],
        scratch_of(receivers) + sums + taken + [own_shape],
        in_place=1,
    )
    inner = permute(inner, lambda i, j: (i ^ blocks, j))
    ends, halo = call(
        functools.partial(mirror_kernel, blocks),
        [offsets, high, low, mirror_weights, near, far, ends, right],
        [ends_shape, (4, held, width + samples)],
        scratch_of(2) + taken + [(4, held, samples)],
        in_place=1,
    )
    ends = permute(ends, lambda i, j: (i ^ blocks, j))
    (own_part,) = call(
        functools.partial(own_kernel, slots, blocks),
        [offsets, high, low, weights, right, halo, recorded, inner, here_spectra, one_spectra]
        + heres_ones,
        [recorded.shape],
        scratch_of(receivers + 2) + sums + taken + [own_shape],
        in_place=1,
    )
    (out,) = call(last_kernel, [own_part, ends], [recorded.shape], [])
    return out


def solution(mesh):
    in_specs = (
        P("rcv", "src", None),
        P("rcv", "src", None),
        P("rcv", "src", None),
        P(None, None, "rcv", "src"),
        P(),
    )
    out_specs = P("rcv", "src", None)
    body = functools.partial(local, mesh.shape["rcv"], mesh.shape["src"])
    return jax.shard_map(body, mesh=mesh, in_specs=in_specs, out_specs=out_specs, check_vma=False)
```
